256 devices in a mesh: corpus: 128 (over y_lo, z, x, core), rep: 2 (over y_hi).
Axes of the slice: x: 4, y: 4 (y_hi: 2, y_lo: 2; y = y_hi * 2 + y_lo), z: 8, core: 2. Of those that a mesh axis runs over, the one named last changes fastest.
Arguments:
- embeddings: bfloat16 [262144, 1024], P(('corpus', 'rep')), may hold values from -6 to 6
- assignments: int32 [262144], P(('corpus', 'rep')), may hold values from 0 to 2047
- old_centroids: bfloat16 [2048, 1024], P('corpus'), may hold values from -6 to 6
- old_counts: int32 [2048], P('corpus'), may hold values from 1 to 32
Outputs:
- residuals: bfloat16 [262144, 1024], P(('corpus', 'rep'))
- new_centroids: bfloat16 [2048, 1024], P('corpus')
The draws below stay inside these ranges and needn't reach their ends.
All inputs are finite; a program needn't handle non-finite values.
Results may differ from the reference program's by a relative error of at most 0.0043.
Values may be sent and summed in bfloat16 or wider, within the bound.
A program may use at most 64 MiB of HBM per device.

```python
import math
import jax
import jax.numpy as jnp
import numpy as np
from jax import lax

D = 1024
CENTROIDS = 2048
TOKENS = 262144


def with_ends(entries, own_key, low, largest):
    spot = [jax.random.randint(jax.random.fold_in(own_key, axis), (), 0, length) for axis, length in enumerate(entries.shape)]
    longest = entries.shape.index(max(entries.shape))
    next_to = spot[:longest] + [(spot[longest] + 1) % entries.shape[longest]] + spot[longest + 1:]
    return entries.at[tuple(spot)].set(low).at[tuple(next_to)].set(largest)


def levels(own_key, shape, pieces, smallest, top_value):
    def one(dim, parts):
        heights = jax.random.uniform(jax.random.fold_in(jax.random.fold_in(own_key, 6), dim), (parts,), jnp.float32, smallest / len(pieces), top_value / len(pieces))
        return jnp.repeat(jnp.exp(heights), shape[dim] // parts).reshape((-1,) + (1,) * (len(shape) - dim - 1))

    loudness = one(*pieces[0])
    for cut in pieces[1:]:
        loudness = loudness * one(*cut)
    return loudness


def cumulative_ranks(count, slope):
    weights = [(1 << 20) // math.isqrt(rank ** slope) + 1 for rank in range(1, count + 1)]
    spread = 1 + sum(weights) // (1 << 30)
    return np.cumsum(np.array([max(1, weight // spread) for weight in weights]))


def skewed_ids(own_key, shape, number_of, slope):
    listing = cumulative_ranks(number_of, slope)
    ticket = jax.random.randint(jax.random.fold_in(own_key, 1), shape, 0, int(listing[number_of - 1]))
    rank = jnp.searchsorted(jnp.asarray(listing, jnp.int32), ticket, side="right")
    return jax.random.permutation(jax.random.fold_in(own_key, 2), number_of)[rank].astype(jnp.int32)


def centred(stream_key, dims, scale, reach, pieces=(), kind=jnp.bfloat16):
    level = levels(stream_key, dims, pieces, -0.22, 0.18) if pieces else 1.0
    values = jax.random.normal(stream_key, dims, jnp.float32) * scale * level
    return jnp.minimum(jnp.maximum(values, -reach), reach).astype(kind)


def setup_inputs(seed: int = 0) -> dict:
    arg_keys = jax.random.split(jax.random.key(seed), 5)
    return {
        "embeddings": centred(arg_keys[0], (TOKENS, D), 1.0, 6.0, ((0, 256),)),
        "assignments": with_ends(skewed_ids(arg_keys[1], (TOKENS,), CENTROIDS, 1), jax.random.fold_in(arg_keys[1], 3), 0, CENTROIDS - 1).astype(jnp.int32),
        "old_centroids": centred(arg_keys[2], (CENTROIDS, D), 1.0, 6.0, ((0, 128),)),
        "old_counts": with_ends(jax.random.randint(arg_keys[3], (CENTROIDS,), 1, 33), jax.random.fold_in(arg_keys[3], 1), 1, 32).astype(jnp.int32),
    }


def block_sums(total, block):
    rows, labels = block
    return (total + jax.ops.segment_sum(rows.astype(jnp.float32), labels, num_segments=CENTROIDS), None)

def reference(embeddings, assignments, old_centroids, old_counts):
    step_rows = min(TOKENS, 8192)
    blocks = TOKENS // step_rows
    rows = embeddings.reshape(blocks, step_rows, D)
    labels = assignments.reshape(blocks, step_rows)
    sums, unused = lax.scan(block_sums, jnp.zeros((CENTROIDS, D), jnp.float32), (rows, labels))
    merged = old_counts.astype(jnp.float32)[:, None] * old_centroids.astype(jnp.float32) + sums
    scale = lax.rsqrt(lax.optimization_barrier(jnp.mean(merged * merged, axis=1, keepdims=True)) + 1e-06)
    new_centroids = (merged * scale).astype(jnp.bfloat16)
    picked = jnp.take(new_centroids, assignments, axis=0)
    residuals = (embeddings.astype(jnp.float32) - picked.astype(jnp.float32)).astype(jnp.bfloat16)
    return (residuals, new_centroids)
```

```python
import jax
import jax.numpy as jnp
from jax import lax
from jax.experimental import pallas as pl
from jax.experimental.pallas import tpu as pltpu
from jax.sharding import PartitionSpec as P

MESH = pl.DeviceIdType.MESH
F32, BF16, I32 = jnp.float32, jnp.bfloat16, jnp.int32

RING, DEPTH, ROWS = 4, 8, 16
QB = DEPTH * ROWS
PB = RING * QB
NSEM = 72


def place():
    c, r = lax.axis_index("corpus"), lax.axis_index("rep")
    core, x, z, ylo = c % 2, (c // 2) % RING, (c // (2 * RING)) % DEPTH, c // (2 * RING * DEPTH)
    return core, x, r * 2 + ylo, z, r


def device(core, x, y, z):
    return (((y % 2) * DEPTH + z) * RING + x) * 2 + core, y // 2


def label_of(i, core, x, y, z):
    p0, q0 = x + core * (y - x), y + core * (x - y)
    p = (p0 + (i >> 9)) & 3
    q = (q0 + ((i >> 7) & 3)) & 3
    zz = (z + ((i >> 4) & 7)) & 7
    xx, yy = p + core * (q - p), q + core * (p - q)
    return (((((yy & 1) * DEPTH + zz) * RING + xx) * 2 + (yy >> 1)) << 4) + (i & 15)


def kernel(
    emb, asg, old, cnt, out, new_out,
    own, sib, oth, asg_sib, oldx, oldx_in,
    send_p, recv_p, part, red,
    send_q, recv_q, red_q, send_z, recv_z,
    ss_out, ss_in, tab, tab_sib, asg_t, hot, hot_sib, acc, acc_sib, res, res_sib,
    send_sems, recv_sems, local_sems,
):
    core, x, y, z, r = place()
    tokens, half = own.shape
    swap = 1 - core
    p0, q0 = x + core * (y - x), y + core * (x - y)

    def pq(p, q):
        p, q = lax.rem(p + RING, RING), lax.rem(q + RING, RING)
        return device(core, p + core * (q - p), q + core * (p - q), z)

    sibling = device(swap, x, y, z)
    right, left = pq(p0 + 1, q0), pq(p0 - 1, q0)
    up, down = pq(p0, q0 + 1), pq(p0, q0 - 1)
    peers = [device(core, x, y, lax.rem(z + k, DEPTH)) for k in range(1, DEPTH)]

    barrier = pltpu.get_barrier_semaphore()
    everyone = [sibling, right, left, up, down] + peers
    for other in everyone:
        pl.semaphore_signal(barrier, inc=1, device_id=other, device_id_type=MESH)

    mine = pl.ds(pl.multiple_of(core * half, 128), half)
    theirs = pl.ds(pl.multiple_of(swap * half, 128), half)
    load_own = pltpu.make_async_copy(emb.at[:, mine], own, local_sems.at[0])
    load_oth = pltpu.make_async_copy(emb.at[:, theirs], oth, local_sems.at[1])
    load_own.start()
    load_oth.start()

    eye = lax.broadcasted_iota(I32, (ROWS, ROWS), 0) == lax.broadcasted_iota(I32, (ROWS, ROWS), 1)
    weight = jnp.sum(jnp.where(eye, cnt[...].astype(F32), 0.0), axis=1, keepdims=True)
    oldx[...] = weight * old[:, theirs].astype(F32)

    pending = []

    def send(src, dst, to):
        n = len(pending)
        copy = pltpu.make_async_remote_copy(
            src_ref=src, dst_ref=dst, send_sem=send_sems.at[n], recv_sem=recv_sems.at[n],
            device_id=to, device_id_type=MESH,
        )
        copy.start()
        pending.append(copy)
        return copy

    pl.semaphore_wait(barrier, len(everyone))
    got_emb = send(emb.at[:, theirs], sib, sibling)
    got_asg = send(asg, asg_sib, sibling)
    got_old = send(oldx, oldx_in, sibling)

    hb = PB // 2
    ready = []

    def chunk(relp, h):
        i = lax.broadcasted_iota(I32, (hb, 1), 0) + (relp * PB + h * hb)
        labels = label_of(i, core, x, y, z)
        if not ready:
            load_own.wait()
        mine_hot = (labels == asg[...]).astype(F32).astype(BF16)
        total = jnp.dot(mine_hot, own[...], preferred_element_type=F32)
        if not ready:
            got_asg.wait_recv()
            got_emb.wait_recv()
            ready.append(True)
        their_hot = (labels == asg_sib[...]).astype(F32).astype(BF16)
        return total + jnp.dot(their_hot, sib[...], preferred_element_type=F32)

    send_p[0] = chunk(2, 0).astype(BF16)
    r1 = send(send_p.at[0], recv_p.at[0], right)
    send_p[1] = chunk(2, 1).astype(BF16)
    l1 = send(send_p.at[1], recv_p.at[1], left)
    send_p[2] = chunk(1, 1).astype(BF16)
    r2 = send(send_p.at[2], recv_p.at[2], right)
    send_p[3] = chunk(3, 0).astype(BF16)
    l2 = send(send_p.at[3], recv_p.at[3], left)
    part[0] = chunk(1, 0)
    part[1] = chunk(3, 1)
    r1.wait_recv()
    send_p[4] = (part[0] + recv_p[0].astype(F32)).astype(BF16)
    r3 = send(send_p.at[4], recv_p.at[4], right)
    l1.wait_recv()
    send_p[5] = (part[1] + recv_p[1].astype(F32)).astype(BF16)
    l3 = send(send_p.at[5], recv_p.at[5], left)
    red[0:hb, :] = chunk(0, 0)
    red[hb:PB, :] = chunk(0, 1)

    for t in range(tokens // 128):
        row = jnp.broadcast_to(asg[:, t * 128 : (t + 1) * 128], (128, 128))
        asg_t[t * 128 : (t + 1) * 128, :] = row.T

    def fill(b, carry):
        i = lax.broadcasted_iota(I32, (1, 128), 1) + b * 128
        lanes = pl.ds(pl.multiple_of(b * 128, 128), 128)
        hot[:, lanes] = (asg_t[...] == label_of(i, core, x, y, z)).astype(F32).astype(BF16)
        hot_sib[:, lanes] = (asg_t[...] == label_of(i, swap, x, y, z)).astype(F32).astype(BF16)
        return carry

    lax.fori_loop(0, RING * PB // 128, fill, 0)

    r2.wait_recv()
    l3.wait_recv()
    red[hb:PB, :] = red[hb:PB, :] + (recv_p[2].astype(F32) + recv_p[5].astype(F32))
    hq = QB // 2

    def piece(relq, h):
        return red[relq * QB + h * hq : relq * QB + (h + 1) * hq, :]

    send_q[0] = piece(2, 0).astype(BF16)
    r1 = send(send_q.at[0], recv_q.at[0], up)
    send_q[1] = piece(2, 1).astype(BF16)
    l1 = send(send_q.at[1], recv_q.at[1], down)
    send_q[3] = piece(3, 0).astype(BF16)
    down2 = send(send_q.at[3], recv_q.at[3], down)
    l2.wait_recv()
    r3.wait_recv()
    red[0:hb, :] = red[0:hb, :] + (recv_p[3].astype(F32) + recv_p[4].astype(F32))
    send_q[2] = piece(1, 1).astype(BF16)
    up2 = send(send_q.at[2], recv_q.at[2], up)
    r1.wait_recv()
    send_q[4] = (piece(1, 0) + recv_q[0].astype(F32)).astype(BF16)
    up3 = send(send_q.at[4], recv_q.at[4], up)
    l1.wait_recv()
    send_q[5] = (piece(3, 1) + recv_q[1].astype(F32)).astype(BF16)
    down3 = send(send_q.at[5], recv_q.at[5], down)
    down2.wait_recv()
    up2.wait_recv()
    up3.wait_recv()
    red_q[0:hq, :] = piece(0, 0) + (recv_q[3].astype(F32) + recv_q[4].astype(F32))
    down3.wait_recv()
    red_q[hq:QB, :] = piece(0, 1) + (recv_q[2].astype(F32) + recv_q[5].astype(F32))

    send_z[...] = red_q[...].astype(BF16)
    zs = [
        send(send_z.at[k * ROWS : (k + 1) * ROWS, :], recv_z.at[k * ROWS : (k + 1) * ROWS, :], peers[k - 1])
        for k in range(1, DEPTH)
    ]
    got_old.wait_recv()
    stale = jnp.where(core == r, weight * old[:, mine].astype(F32), oldx_in[...])
    merged = red_q[0:ROWS, :] + stale
    for k in range(1, DEPTH):
        zs[k - 1].wait_recv()
        merged = merged + recv_z[k * ROWS : (k + 1) * ROWS, :].astype(F32)

    ss_out[...] = jnp.broadcast_to(jnp.sum(merged * merged, axis=1, keepdims=True), (ROWS, 128))
    got_ss = send(ss_out, ss_in, sibling)
    got_ss.wait_recv()
    mean = (ss_out[:, 0:1] + ss_in[:, 0:1]) * (1.0 / (2 * half))
    tab[0:ROWS, :] = (merged * lax.rsqrt(mean + 1e-6)).astype(BF16)

    zs = [
        send(tab.at[0:ROWS, :], tab.at[(DEPTH - k) * ROWS : (DEPTH - k + 1) * ROWS, :], peers[k - 1])
        for k in range(1, DEPTH)
    ]
    for copy in zs:
        copy.wait_recv()

    def rows(relp, relq, h=None):
        start = relp * PB + relq * QB
        if h is None:
            return tab.at[start : start + QB, :]
        return tab.at[start + h * hq : start + (h + 1) * hq, :]

    from_left, from_right = {}, {}

    def first_ring(relq):
        from_left[relq] = send(rows(0, relq), rows(3, relq), right)
        from_right[relq] = send(rows(0, relq), rows(1, relq), left)

    q_up = send(rows(0, 0), rows(0, 3), up)
    q_down = send(rows(0, 0), rows(0, 1), down)
    first_ring(0)
    q_up.wait_recv()
    f_up = send(rows(0, 3, 0), rows(0, 2, 0), up)
    first_ring(3)
    q_down.wait_recv()
    f_down = send(rows(0, 1, 1), rows(0, 2, 1), down)
    first_ring(1)
    f_up.wait_recv()
    f_down.wait_recv()
    first_ring(2)

    def pass_on(start, count):
        return send(tab.at[start : start + count, :], tab_sib.at[start : start + count, :], sibling)

    step = 256

    def look(total, which, table, spans, first):
        def body(t, carry):
            tok = pl.ds(pl.multiple_of(t * step, step), step)
            picked = [
                jnp.dot(which[tok, a : a + n], table[a : a + n, :], preferred_element_type=F32) for a, n in spans
            ]
            value = sum(picked[1:], picked[0])
            total[tok, :] = value if first else total[tok, :] + value
            return carry

        lax.fori_loop(0, tokens // step, body, 0)

    sib0 = pass_on(0, PB)
    look(acc, hot, tab, [(0, PB)], True)

    forwards = []
    from_left[0].wait_recv()
    forwards.append(send(rows(3, 0), rows(2, 0), right))
    from_right[0].wait_recv()
    from_right[3].wait_recv()
    forwards.append(send(rows(1, 3), rows(2, 3), left))
    from_left[3].wait_recv()
    from_left[1].wait_recv()
    forwards.append(send(rows(3, 1), rows(2, 1), right))
    from_right[1].wait_recv()
    from_right[2].wait_recv()
    forwards.append(send(rows(1, 2), rows(2, 2), left))
    sib1 = pass_on(PB, PB)
    from_left[2].wait_recv()
    sib3 = pass_on(3 * PB, PB)
    sib0.wait_recv()
    look(acc_sib, hot_sib, tab_sib, [(0, PB)], True)
    look(acc, hot, tab, [(PB, PB), (3 * PB, PB)], False)
    for copy in forwards:
        copy.wait_recv()
    sib2 = pass_on(2 * PB, PB)
    sib1.wait_recv()
    sib3.wait_recv()
    look(acc_sib, hot_sib, tab_sib, [(PB, PB), (3 * PB, PB)], False)
    load_oth.wait()

    stores = []

    def finish(result, total, which, table, passages, columns, sem):
        for t in range(tokens // step):
            tok = slice(t * step, (t + 1) * step)
            picked = jnp.dot(which[tok, 2 * PB : 3 * PB], table[2 * PB : 3 * PB, :], preferred_element_type=F32)
            result[tok, :] = (passages[tok, :].astype(F32) - (total[tok, :] + picked)).astype(BF16)
            store = pltpu.make_async_copy(result.at[tok, :], out.at[tok, columns], local_sems.at[sem + t])
            store.start()
            stores.append(store)

    finish(res, acc, hot, tab, own, mine, 4)
    sib2.wait_recv()
    finish(res_sib, acc_sib, hot_sib, tab_sib, oth, theirs, 8)

    away = lax.rem(core + r, 2) * 2
    a = pl.multiple_of(away * (QB + core * (PB - QB)), ROWS)
    b = pl.multiple_of(away * (QB + swap * (PB - QB)), ROWS)
    left_half = pltpu.make_async_copy(tab.at[pl.ds(a, ROWS), :], new_out.at[:, mine], local_sems.at[2])
    right_half = pltpu.make_async_copy(tab_sib.at[pl.ds(b, ROWS), :], new_out.at[:, theirs], local_sems.at[3])
    left_half.start()
    right_half.start()
    for copy in pending:
        copy.wait_send()
    for store in stores:
        store.wait()
    left_half.wait()
    right_half.wait()


def body(embeddings, assignments, old_centroids, old_counts):
    tokens, width = embeddings.shape
    half, table = width // 2, RING * PB
    vmem = pltpu.VMEM
    return pl.pallas_call(
        kernel,
        out_shape=(
            jax.ShapeDtypeStruct((tokens, width), BF16),
            jax.ShapeDtypeStruct((ROWS, width), BF16),
        ),
        in_specs=[
            pl.BlockSpec(memory_space=pl.ANY),
            pl.BlockSpec(memory_space=vmem),
            pl.BlockSpec(memory_space=vmem),
            pl.BlockSpec(memory_space=vmem),
        ],
        out_specs=(pl.BlockSpec(memory_space=pl.ANY), pl.BlockSpec(memory_space=pl.ANY)),
        scratch_shapes=[
            vmem((tokens, half), BF16),
            vmem((tokens, half), BF16),
            vmem((tokens, half), BF16),
            vmem((1, tokens), I32),
            vmem((ROWS, half), F32),
            vmem((ROWS, half), F32),
            vmem((6, PB // 2, half), BF16),
            vmem((6, PB // 2, half), BF16),
            vmem((2, PB // 2, half), F32),
            vmem((PB, half), F32),
            vmem((6, QB // 2, half), BF16),
            vmem((6, QB // 2, half), BF16),
            vmem((QB, half), F32),
            vmem((QB, half), BF16),
            vmem((QB, half), BF16),
            vmem((ROWS, 128), F32),
            vmem((ROWS, 128), F32),
            vmem((table, half), BF16),
            vmem((table, half), BF16),
            vmem((tokens, 128), I32),
            vmem((tokens, table), BF16),
            vmem((tokens, table), BF16),
            vmem((tokens, half), F32),
            vmem((tokens, half), F32),
            vmem((tokens, half), BF16),
            vmem((tokens, half), BF16),
            pltpu.SemaphoreType.DMA((NSEM,)),
            pltpu.SemaphoreType.DMA((NSEM,)),
            pltpu.SemaphoreType.DMA((12,)),
        ],
        compiler_params=pltpu.CompilerParams(
            collective_id=0, has_side_effects=True, vmem_limit_bytes=58 * 1024 * 1024
        ),
        cost_estimate=pl.CostEstimate(flops=8 * 2**30, bytes_accessed=4 * 2**20, transcendentals=0),
    )(embeddings, assignments.reshape(1, tokens), old_centroids, old_counts.reshape(1, ROWS))


def solution(mesh):
    placed = (P(("corpus", "rep"), None), P(("corpus", "rep")), P("corpus", None), P("corpus"))
    return jax.shard_map(
        body,
        mesh=mesh,
        in_specs=placed,
        out_specs=(P(("corpus", "rep"), None), P("corpus", None)),
        check_vma=False,
    )
```

```python
import jax
import jax.numpy as jnp
from jax import lax
from jax.experimental import pallas as pl
from jax.experimental.pallas import tpu as pltpu
from jax.sharding import PartitionSpec as P

MESH = pl.DeviceIdType.MESH
F32, BF16, I32, I16 = jnp.float32, jnp.bfloat16, jnp.int32, jnp.int16

RING, DEPTH, ROWS = 4, 8, 16
PIECE = DEPTH // 2 * ROWS
HALF = RING * PIECE
PB = 2 * HALF
HOME = 5
TOP = ROWS // 2


def place():
    c, r = lax.axis_index("corpus"), lax.axis_index("rep")
    core, x, z, ylo = c % 2, (c // 2) % RING, (c // (2 * RING)) % DEPTH, c // (2 * RING * DEPTH)
    return core, x, r * 2 + ylo, z, r


def device(core, x, y, z):
    return (((y % 2) * DEPTH + z) * RING + x) * 2 + core, y // 2


def label_of(i, core, x, y, z):
    p0, q0 = x + core * (y - x), y + core * (x - y)
    p = (p0 + (i >> 9)) & 3
    q = (q0 + 3 - ((i >> 6) & 3)) & 3
    zz = (z + 3 + ((i >> 4) & 3) + ((i >> 6) & 4)) & 7
    xx, yy = p + core * (q - p), q + core * (p - q)
    return (((((yy & 1) * DEPTH + zz) * RING + xx) * 2 + (yy >> 1)) << 4) + (i & 15)


def label_parts(i, core, x, y, z):
    q = ((y + core * (x - y)) + 3 - ((i >> 6) & 3)) & 3
    zz = (z + 3 + ((i >> 4) & 3) + ((i >> 6) & 4)) & 7
    first = ((((q & 1) * DEPTH + zz) * RING * 2 + (q >> 1)) << 4) + (i & 15)
    second = (((zz * RING + q) * 2) << 4) + (i & 15)
    return first + core * (second - first)


def shift_of(p, core):
    first = p * 2 * ROWS
    second = (p % 2) * (DEPTH * RING * 2 * ROWS) + (p // 2) * ROWS
    return first + core * (second - first)


def spot(relp, zh, qs):
    return relp * PB + zh * HALF + qs * PIECE


def kernel(
    emb, asg_in, old_in, cnt_in, out, new_out,
    own, sib, oth, asg, asg_sib, old, cnt, prod, old_sib,
    labels, hot_p, send_p, recv_p, part, send_q, recv_q, send_z, recv_z, send_g, recv_g,
    tab, tab_sib, asg_t, hot, hot_sib,
    load_sems, send_sems, swap_sems, near_sems, far_sems, ring_sems, across_sems, line_sems,
    gather_sems, pass_sems, share_sems,
):
    core, x, y, z, r = place()
    tokens, half = own.shape
    swap = 1 - core
    p0, q0 = x + core * (y - x), y + core * (x - y)

    def pq(p, q):
        p, q = lax.rem(p, RING), lax.rem(q, RING)
        return device(core, p + core * (q - p), q + core * (p - q), z)

    sibling = device(swap, x, y, z)
    right, left = pq(p0 + 1, q0), pq(p0 + 3, q0)
    around = [None] + [pq(p0, q0 + d) for d in range(1, RING)]
    line = {
        (k, c): device(swap if c else core, x, y, lax.rem(z + k, DEPTH))
        for k in range(DEPTH) for c in range(2) if k + c
    }

    barrier = pltpu.get_barrier_semaphore()
    everyone = [right, left] + around[1:] + [line[key] for key in line]
    for other in everyone:
        pl.semaphore_signal(barrier, inc=1, device_id=other, device_id_type=MESH)

    mine = pl.ds(pl.multiple_of(core * half, 128), half)
    theirs = pl.ds(pl.multiple_of(swap * half, 128), half)
    loads = [
        pltpu.make_async_copy(a, b, load_sems.at[n])
        for n, (a, b) in enumerate(
            [(asg_in, asg), (emb.at[:, mine], own), (old_in, old), (cnt_in, cnt), (emb.at[:, theirs], oth)]
        )
    ]
    for load in loads:
        load.start()

    def send(src, dst, to, group, sem):
        copy = pltpu.make_async_remote_copy(
            src_ref=src, dst_ref=dst, send_sem=send_sems.at[group], recv_sem=sem,
            device_id=to, device_id_type=MESH,
        )
        copy.start()
        return copy

    def drain(ref, sem):
        pltpu.make_async_copy(ref, ref, sem).wait()

    pl.semaphore_wait(barrier, len(everyone))
    got_asg = send(asg_in, asg_sib, sibling, 0, swap_sems.at[0])
    got_emb = send(emb.at[:, theirs], sib, sibling, 1, swap_sems.at[1])

    i = lax.broadcasted_iota(I32, (PB, 128), 0)
    labels[...] = label_parts(i, core, x, y, z).astype(I16)
    loads[0].wait()
    loads[1].wait()
    one, zero = jnp.bfloat16(1), jnp.bfloat16(0)

    def chunk(relp, zh, first=False):
        shift = shift_of(lax.rem(p0 + relp, RING), core)
        wanted = labels[zh * HALF : (zh + 1) * HALF, :]

        def hot_rows(ids, base):
            moved = (ids[...] - shift).astype(I16)
            for t in range(0, tokens, 128):
                hot_p[:, base + t : base + t + 128] = jnp.where(wanted == moved[:, t : t + 128], one, zero)

        hot_rows(asg, 0)
        total = jnp.dot(hot_p[:, 0:tokens], own[...], preferred_element_type=F32)
        if first:
            got_asg.wait_recv()
        hot_rows(asg_sib, tokens)
        if first:
            got_emb.wait_recv()
        return total + jnp.dot(hot_p[:, tokens : 2 * tokens], sib[...], preferred_element_type=F32)

    def band(qs):
        return slice(qs * PIECE, (qs + 1) * PIECE)

    def ring(n, to, qs, sem):
        return send(send_p.at[n, band(qs), :], recv_p.at[n, band(qs), :], to, 2, sem)

    send_p[0] = chunk(2, 0, True).astype(BF16)
    r1 = [ring(0, right, qs, near_sems.at[qs]) for qs in range(RING)]
    send_p[1] = chunk(2, 1).astype(BF16)
    l1 = [ring(1, left, qs, near_sems.at[RING + qs]) for qs in range(RING)]
    send_p[2] = chunk(1, 1).astype(BF16)
    for qs in range(RING):
        ring(2, right, qs, far_sems.at[0])
    send_p[3] = chunk(3, 0).astype(BF16)
    for qs in range(RING):
        ring(3, left, qs, far_sems.at[1])
    part[0] = chunk(1, 0)
    part[1] = chunk(3, 1)
    r3, l3 = [], []
    for copies, arrived, n, to in ((r3, r1, 0, right), (l3, l1, 1, left)):
        for qs in range(RING):
            arrived[qs].wait_recv()
            send_p[4 + n, band(qs), :] = (part[n, band(qs), :] + recv_p[n, band(qs), :].astype(F32)).astype(BF16)
            copies.append(ring(4 + n, to, qs, ring_sems.at[n * RING + qs]))
    part[2] = chunk(0, 0)
    part[3] = chunk(0, 1)

    loads[2].wait()
    loads[3].wait()
    eye = lax.broadcasted_iota(I32, (ROWS, ROWS), 0) == lax.broadcasted_iota(I32, (ROWS, ROWS), 1)
    weight = jnp.sum(jnp.where(eye, cnt[...].astype(F32), 0.0), axis=1, keepdims=True)
    prod[...] = weight * old[...].astype(F32)
    my_rows = pl.ds(pl.multiple_of(core * TOP, TOP), TOP)
    their_rows = pl.ds(pl.multiple_of(swap * TOP, TOP), TOP)
    got_old = send(prod.at[their_rows, :], old_sib, sibling, 3, swap_sems.at[2])

    for t in range(0, tokens, 128):
        row = jnp.broadcast_to(asg[:, t : t + 128], (128, 128))
        asg_t[t : t + 128, :] = row.T.astype(I16)

    def fill(low, high):
        def lanes_of(b, carry):
            i = lax.broadcasted_iota(I32, (ROWS, 128), 1) + b * 128
            lanes = pl.ds(pl.multiple_of(b * 128, 128), 128)
            for ref, which in ((hot, core), (hot_sib, swap)):
                row = label_of(i, which, x, y, z).astype(I16)
                ref[:, lanes] = jnp.where(asg_t[...] == row[0:1, :], one, zero)
            return carry

        lax.fori_loop(low, high, lanes_of, 0)

    fill(0, 8)

    drain(recv_p.at[2], far_sems.at[0])
    drain(recv_p.at[3], far_sems.at[1])

    def whole(zh, qs):
        (r3, l3)[zh][qs].wait_recv()
        m, n = (4, 3) if zh == 0 else (5, 2)
        return part[2 + zh, band(qs), :] + (recv_p[m, band(qs), :].astype(F32) + recv_p[n, band(qs), :].astype(F32))

    for zh in range(2):
        for qs in range(RING - 1):
            send_q[zh, band(qs), :] = whole(zh, qs).astype(BF16)
            send(send_q.at[zh, band(qs), :], recv_q.at[zh, band(qs), :], around[3 - qs], 4, across_sems.at[zh])
        part[2 + zh, band(3), :] = whole(zh, 3)

    lower = core == 0

    def fold(v):
        return jnp.concatenate([v[:, : half // 2], v[:, half // 2 :]], axis=0)

    def unfold(v):
        return jnp.concatenate([v[:TOP], v[TOP:]], axis=1)

    home = None
    for zh in range(2):
        value = part[2 + zh, band(3), :]
        drain(recv_q.at[zh, 0 : 3 * PIECE, :], across_sems.at[zh])
        for qs in range(RING - 1):
            value = value + recv_q[zh, band(qs), :].astype(F32)
        for j in range(4):
            k = (zh * 4 + j + 3) % DEPTH
            low, high = value[j * ROWS : j * ROWS + TOP, :], value[j * ROWS + TOP : (j + 1) * ROWS, :]
            for c, v in ((0, jnp.where(lower, low, high)), (1, jnp.where(lower, high, low))):
                if k + c == 0:
                    home = fold(v)
                    continue
                send_z[2 * k + c] = fold(v).astype(BF16)
                send(send_z.at[2 * k + c], recv_z.at[(DEPTH - k) % DEPTH * 2 + c], line[k, c], 5, line_sems.at[0])
    fill(8, 11)
    got_old.wait_recv()
    drain(recv_z.at[1:], line_sems.at[0])
    other = recv_z[1].astype(F32)
    for k in range(1, DEPTH):
        home = home + recv_z[2 * k].astype(F32)
        other = other + recv_z[2 * k + 1].astype(F32)
    held = core == r
    home = unfold(home) + jnp.where(held, prod[my_rows, mine], old_sib[:, mine])
    other = unfold(other) + jnp.where(held, prod[my_rows, theirs], old_sib[:, theirs])
    squares = jnp.sum(home * home, axis=1, keepdims=True) + jnp.sum(other * other, axis=1, keepdims=True)
    scale = lax.rsqrt(squares * (1.0 / (2 * half)) + 1e-6)
    fresh = fold(home * scale).astype(BF16)
    send_g[0] = fresh
    send_g[1] = fold(other * scale).astype(BF16)
    recv_g[0] = fresh

    for k in (4, 3, 5, 2, 6, 1, 7, 0):
        for c in range(2):
            if k + c:
                zh = (HOME - k) % DEPTH // 4
                send(send_g.at[c], recv_g.at[(DEPTH - k) % DEPTH * 2 + c], line[k, c], 6, line_sems.at[1 + zh])
    fill(11, 16)

    def piece(ref, relp, zh, qs):
        start = spot(relp, zh, qs)
        return ref.at[start : start + PIECE, :]

    across, from_left, from_right = {}, {}, {}

    def share(relp, zh, qs):
        send(piece(tab, relp, zh, qs), piece(tab_sib, relp, zh, qs), sibling, 7, share_sems.at[relp])

    def first_ring(zh, qs):
        n = zh * RING + qs
        from_left[zh, qs] = send(piece(tab, 0, zh, qs), piece(tab, 3, zh, qs), right, 8, gather_sems.at[n])
        from_right[zh, qs] = send(piece(tab, 0, zh, qs), piece(tab, 1, zh, qs), left, 8, gather_sems.at[8 + n])
        share(0, zh, qs)

    def pass_on(zh, qs):
        goes_right = (zh + qs) % 2 == 0
        for arrived, relp, to in ((from_left, 3, right), (from_right, 1, left)):
            arrived[zh, qs].wait_recv()
            if (relp == 3) == goes_right:
                send(piece(tab, relp, zh, qs), piece(tab, 2, zh, qs), to, 9, pass_sems.at[zh])
            share(relp, zh, qs)

    for zh in (1, 0):
        drain(recv_g.at[0 : 8 - zh], line_sems.at[1 + zh])
        for j in range(4):
            k = (zh * 4 + j + 3) % DEPTH
            same, sister = unfold(recv_g[2 * k].astype(F32)), unfold(recv_g[2 * k + 1].astype(F32))
            block = jnp.concatenate([jnp.where(lower, same, sister), jnp.where(lower, sister, same)], axis=0)
            start = spot(0, zh, 3) + j * ROWS
            tab[start : start + ROWS, :] = block.astype(BF16)
        for d in (2, 1, 3):
            n = zh * 3 + d - 1
            across[zh, d] = send(
                piece(tab, 0, zh, 3), piece(tab, 0, zh, d - 1), around[d], 10, across_sems.at[2 + n]
            )
        first_ring(zh, 3)
    for zh in (1, 0):
        for d in (1, 3, 2):
            across[zh, d].wait_recv()
            first_ring(zh, d - 1)
        pass_on(zh, 3)

    step = 256

    def look(state, which, table, spans):
        def tile(t, carry):
            tok = pl.ds(pl.multiple_of(t * step, step), step)
            picked = [
                jnp.dot(which[tok, a : a + n], table[a : a + n, :], preferred_element_type=F32) for a, n in spans
            ]
            state[tok, :] = (state[tok, :].astype(F32) - sum(picked[1:], picked[0])).astype(BF16)
            return carry

        lax.fori_loop(0, tokens // step, tile, 0)

    look(own, hot, tab, [(0, PB)])
    loads[4].wait()
    drain(tab.at[0:PB, :], share_sems.at[0])
    look(oth, hot_sib, tab_sib, [(0, PB)])
    for zh in (1, 0):
        for qs in (0, 2, 1):
            pass_on(zh, qs)
    look(own, hot, tab, [(PB, PB), (3 * PB, PB)])
    drain(asg, send_sems.at[0])
    drain(own, send_sems.at[1])
    drain(send_p, send_sems.at[2])
    drain(old_sib, send_sems.at[3])
    drain(send_q.at[:, 0 : 3 * PIECE, :], send_sems.at[4])
    drain(send_z.at[1:], send_sems.at[5])
    drain(send_z.at[1:], send_sems.at[6])
    drain(tab.at[0 : 2 * PB, :], send_sems.at[8])
    drain(tab.at[0 : 6 * PIECE, :], send_sems.at[10])
    drain(tab.at[0:PB, :], share_sems.at[1])
    drain(tab.at[0:PB, :], share_sems.at[3])
    look(oth, hot_sib, tab_sib, [(PB, PB), (3 * PB, PB)])
    last = []
    for zh in (1, 0):
        drain(tab.at[0:HALF, :], pass_sems.at[zh])
        start = spot(2, zh, 0)
        last.append(
            send(tab.at[start : start + HALF, :], tab_sib.at[start : start + HALF, :], sibling, 11 + zh, pass_sems.at[2 + zh])
        )

    def finish(state, which, table, columns):
        def tile(t, carry):
            tok = pl.ds(pl.multiple_of(t * step, step), step)
            picked = jnp.dot(which[tok, 2 * PB : 3 * PB], table[2 * PB : 3 * PB, :], preferred_element_type=F32)
            out[tok, columns] = (state[tok, :].astype(F32) - picked).astype(BF16)
            return carry

        lax.fori_loop(0, tokens // step, tile, 0)

    finish(own, hot, tab, mine)
    for copy in last:
        copy.wait_recv()
    finish(oth, hot_sib, tab_sib, theirs)

    away = lax.rem(core + r, 2) * 2
    base = HALF + (HOME - 4) * ROWS
    a = base + swap * (3 - away) * PIECE + core * (away * PB + 3 * PIECE)
    b = base + core * (3 - away) * PIECE + swap * (away * PB + 3 * PIECE)
    new_out[:, mine] = tab[pl.ds(pl.multiple_of(a, ROWS), ROWS), :]
    new_out[:, theirs] = tab_sib[pl.ds(pl.multiple_of(b, ROWS), ROWS), :]
    drain(tab.at[0 : 3 * PB, :], send_sems.at[7])
    drain(tab.at[0:PB, :], send_sems.at[9])
    for copy in last:
        copy.wait_send()


def body(embeddings, assignments, old_centroids, old_counts):
    tokens, width = embeddings.shape
    half, table = width // 2, RING * PB
    vmem, dma = pltpu.VMEM, pltpu.SemaphoreType.DMA
    operands = (embeddings, assignments.reshape(1, tokens), old_centroids, old_counts.reshape(1, ROWS))
    hbm = pl.BlockSpec(memory_space=pltpu.HBM)
    return pl.pallas_call(
        kernel,
        out_shape=(vmem((tokens, width), BF16), vmem((ROWS, width), BF16)),
        in_specs=[hbm] * 4,
        out_specs=(pl.BlockSpec(memory_space=vmem), pl.BlockSpec(memory_space=vmem)),
        scratch_shapes=[
            vmem((tokens, half), BF16),
            vmem((tokens, half), BF16),
            vmem((tokens, half), BF16),
            vmem((1, tokens), I32),
            vmem((1, tokens), I32),
            vmem((ROWS, width), BF16),
            vmem((1, ROWS), I32),
            vmem((ROWS, width), F32),
            vmem((TOP, width), F32),
            vmem((PB, 128), I16),
            vmem((HALF, 2 * tokens), BF16),
            vmem((6, HALF, half), BF16),
            vmem((6, HALF, half), BF16),
            vmem((4, HALF, half), F32),
            vmem((2, HALF, half), BF16),
            vmem((2, HALF, half), BF16),
            vmem((2 * DEPTH, ROWS, half // 2), BF16),
            vmem((2 * DEPTH, ROWS, half // 2), BF16),
            vmem((2, ROWS, half // 2), BF16),
            vmem((2 * DEPTH, ROWS, half // 2), BF16),
            vmem((table, half), BF16),
            vmem((table, half), BF16),
            vmem((tokens, 128), I16),
            vmem((tokens, table), BF16),
            vmem((tokens, table), BF16),
            dma((5,)),
            dma((13,)),
            dma((3,)),
            dma((8,)),
            dma((2,)),
            dma((8,)),
            dma((8,)),
            dma((3,)),
            dma((16,)),
            dma((4,)),
            dma((4,)),
        ],
        compiler_params=pltpu.CompilerParams(
            collective_id=0, has_side_effects=True, vmem_limit_bytes=58 * 1024 * 1024
        ),
        cost_estimate=pl.CostEstimate(flops=8 * 2**30, bytes_accessed=4 * 2**20, transcendentals=0),
    )(*[pltpu.with_memory_space_constraint(operand, pltpu.HBM) for operand in operands])


def solution(mesh):
    placed = (P(("corpus", "rep"), None), P(("corpus", "rep")), P("corpus", None), P("corpus"))
    return jax.shard_map(
        body,
        mesh=mesh,
        in_specs=placed,
        out_specs=(P(("corpus", "rep"), None), P("corpus", None)),
        check_vma=False,
    )
```

```python
import jax
import jax.numpy as jnp
from jax import lax
from jax.experimental import pallas as pl
from jax.experimental.pallas import tpu as pltpu
from jax.sharding import PartitionSpec as P

MESH = pl.DeviceIdType.MESH
F32, BF16, I32, I16 = jnp.float32, jnp.bfloat16, jnp.int32, jnp.int16

RING, DEPTH, ROWS = 4, 8, 16
PIECE = DEPTH // 2 * ROWS
HALF = RING * PIECE
PB = 2 * HALF
HOME = 5
TOP = ROWS // 2


def place():
    c, r = lax.axis_index("corpus"), lax.axis_index("rep")
    core, x, z, ylo = c % 2, (c // 2) % RING, (c // (2 * RING)) % DEPTH, c // (2 * RING * DEPTH)
    return core, x, r * 2 + ylo, z, r


def device(core, x, y, z):
    return (((y % 2) * DEPTH + z) * RING + x) * 2 + core, y // 2


def label_of(i, turn, x, y, z):
    p0, q0 = x + turn * (y - x), y + turn * (x - y)
    p = (p0 + (i >> 9)) & 3
    q = (q0 + 3 - ((i >> 6) & 3)) & 3
    zz = (z + 3 + ((i >> 4) & 3) + ((i >> 6) & 4)) & 7
    xx, yy = p + turn * (q - p), q + turn * (p - q)
    return (((((yy & 1) * DEPTH + zz) * RING + xx) * 2 + (yy >> 1)) << 4) + (i & 15)


def label_parts(i, turn, x, y, z):
    q = ((y + turn * (x - y)) + 3 - ((i >> 6) & 3)) & 3
    zz = (z + 3 + ((i >> 4) & 3) + ((i >> 6) & 4)) & 7
    first = ((((q & 1) * DEPTH + zz) * RING * 2 + (q >> 1)) << 4) + (i & 15)
    second = (((zz * RING + q) * 2) << 4) + (i & 15)
    return first + turn * (second - first)


def shift_of(p, turn):
    first = p * 2 * ROWS
    second = (p % 2) * (DEPTH * RING * 2 * ROWS) + (p // 2) * ROWS
    return first + turn * (second - first)


def spot(relp, zh, qs):
    return relp * PB + zh * HALF + qs * PIECE


def kernel(
    emb, asg_in, old_in, cnt_in, out, new_out,
    own, sib, oth, asg, asg_sib, old, cnt, prod, old_sib,
    labels, hot_p, send_p, recv_p, part, send_q, recv_q, send_z, recv_z, send_g, recv_g,
    tab, tab_sib, asg_t, hot, hot_sib,
    load_sems, send_sems, swap_sems, near_sems, far_sems, ring_sems, across_sems, line_sems,
    gather_sems, pass_sems, share_sems,
):
    core, x, y, z, r = place()
    tokens, half = own.shape
    quarter = half // 2
    swap = 1 - core
    turns = (core, swap)
    both = range(2)

    def chip(turn, p, q):
        p, q = lax.rem(p, RING), lax.rem(q, RING)
        return device(core, p + turn * (q - p), q + turn * (p - q), z)

    sibling = device(swap, x, y, z)
    first0 = [x + turn * (y - x) for turn in turns]
    second0 = [y + turn * (x - y) for turn in turns]
    right = [chip(turns[g], first0[g] + 1, second0[g]) for g in both]
    left = [chip(turns[g], first0[g] + 3, second0[g]) for g in both]
    around = [[chip(turns[g], first0[g], second0[g] + d) for d in range(RING)] for g in both]
    line = {
        (k, c): device(swap if c else core, x, y, lax.rem(z + k, DEPTH))
        for k in range(DEPTH) for c in range(2) if k + c
    }

    barrier = pltpu.get_barrier_semaphore()
    everyone = around[0][1:] + around[1][1:] + [line[key] for key in line]
    for other in everyone:
        pl.semaphore_signal(barrier, inc=1, device_id=other, device_id_type=MESH)

    def columns_of(side, g):
        return pl.ds(pl.multiple_of(side * half + g * quarter, 128), quarter)

    mine = pl.ds(pl.multiple_of(core * half, 128), half)
    theirs = pl.ds(pl.multiple_of(swap * half, 128), half)
    loads = [
        pltpu.make_async_copy(a, b, load_sems.at[n])
        for n, (a, b) in enumerate(
            [(asg_in, asg), (emb.at[:, mine], own), (old_in, old), (cnt_in, cnt), (emb.at[:, theirs], oth)]
        )
    ]
    for load in loads:
        load.start()

    def send(src, dst, to, group, sem):
        copy = pltpu.make_async_remote_copy(
            src_ref=src, dst_ref=dst, send_sem=send_sems.at[group], recv_sem=sem,
            device_id=to, device_id_type=MESH,
        )
        copy.start()
        return copy

    def drain(ref, sem):
        pltpu.make_async_copy(ref, ref, sem).wait()

    pl.semaphore_wait(barrier, len(everyone))
    got_asg = send(asg_in, asg_sib, sibling, 0, swap_sems.at[0])
    got_emb = send(emb.at[:, theirs], sib, sibling, 1, swap_sems.at[1])

    i = lax.broadcasted_iota(I32, (PB, 128), 0)
    for g in both:
        labels[g] = label_parts(i, turns[g], x, y, z).astype(I16)
    loads[0].wait()
    loads[1].wait()
    one, zero = jnp.bfloat16(1), jnp.bfloat16(0)

    def chunk(g, relp, zh, first=False):
        shift = shift_of(lax.rem(first0[g] + relp, RING), turns[g])
        wanted = labels[g, zh * HALF : (zh + 1) * HALF, :]
        cols = slice(g * quarter, (g + 1) * quarter)

        def hot_rows(ids, base):
            moved = (ids[...] - shift).astype(I16)
            for t in range(0, tokens, 128):
                hot_p[:, base + t : base + t + 128] = jnp.where(wanted == moved[:, t : t + 128], one, zero)

        hot_rows(asg, 0)
        total = jnp.dot(hot_p[:, 0:tokens], own[:, cols], preferred_element_type=F32)
        if first:
            got_asg.wait_recv()
        hot_rows(asg_sib, tokens)
        if first:
            got_emb.wait_recv()
        return total + jnp.dot(hot_p[:, tokens : 2 * tokens], sib[:, cols], preferred_element_type=F32)

    def band(qs):
        return slice(qs * PIECE, (qs + 1) * PIECE)

    def ring(g, n, to, qs, sem):
        return send(send_p.at[g, n, band(qs), :], recv_p.at[g, n, band(qs), :], to[g], 2, sem)

    early = {}
    for n, relp, zh, to in ((0, 2, 0, right), (1, 2, 1, left), (2, 1, 1, right), (3, 3, 0, left)):
        for g in both:
            send_p[g, n] = chunk(g, relp, zh, n + g == 0).astype(BF16)
            for qs in range(RING):
                sem = near_sems.at[(g * 2 + n) * RING + qs] if n < 2 else far_sems.at[g * 2 + n - 2]
                early[g, n, qs] = ring(g, n, to, qs, sem)
    late = {}
    for n, relp, zh, to in ((0, 1, 0, right), (1, 3, 1, left)):
        for g in both:
            part[g, n] = chunk(g, relp, zh)
        for g in both:
            for qs in range(RING):
                early[g, n, qs].wait_recv()
                summed = part[g, n, band(qs), :] + recv_p[g, n, band(qs), :].astype(F32)
                send_p[g, 4 + n, band(qs), :] = summed.astype(BF16)
                late[g, n, qs] = ring(g, 4 + n, to, qs, ring_sems.at[(g * 2 + n) * RING + qs])
    for zh in range(2):
        for g in both:
            part[g, 2 + zh] = chunk(g, 0, zh)

    loads[2].wait()
    loads[3].wait()
    eye = lax.broadcasted_iota(I32, (ROWS, ROWS), 0) == lax.broadcasted_iota(I32, (ROWS, ROWS), 1)
    weight = jnp.sum(jnp.where(eye, cnt[...].astype(F32), 0.0), axis=1, keepdims=True)
    prod[...] = weight * old[...].astype(F32)
    my_rows = pl.ds(pl.multiple_of(core * TOP, TOP), TOP)
    their_rows = pl.ds(pl.multiple_of(swap * TOP, TOP), TOP)
    got_old = send(prod.at[their_rows, :], old_sib, sibling, 3, swap_sems.at[2])

    for t in range(0, tokens, 128):
        row = jnp.broadcast_to(asg[:, t : t + 128], (128, 128))
        asg_t[t : t + 128, :] = row.T.astype(I16)

    def fill(low, high):
        def lanes_of(b, carry):
            i = lax.broadcasted_iota(I32, (ROWS, 128), 1) + b * 128
            lanes = pl.ds(pl.multiple_of(b * 128, 128), 128)
            for ref, which in ((hot, core), (hot_sib, swap)):
                row = label_of(i, which, x, y, z).astype(I16)
                ref[:, lanes] = jnp.where(asg_t[...] == row[0:1, :], one, zero)
            return carry

        lax.fori_loop(low, high, lanes_of, 0)

    fill(0, 6)

    for g in both:
        for n in range(2):
            drain(recv_p.at[g, 2 + n], far_sems.at[g * 2 + n])

    def whole(g, zh, qs):
        late[g, zh, qs].wait_recv()
        m, n = (4, 3) if zh == 0 else (5, 2)
        arrived = recv_p[g, m, band(qs), :].astype(F32) + recv_p[g, n, band(qs), :].astype(F32)
        return part[g, 2 + zh, band(qs), :] + arrived

    for zh in range(2):
        for g in both:
            for qs in range(RING - 1):
                send_q[g, zh, band(qs), :] = whole(g, zh, qs).astype(BF16)
                send(
                    send_q.at[g, zh, band(qs), :], recv_q.at[g, zh, band(qs), :], around[g][3 - qs], 4,
                    across_sems.at[g * 2 + zh],
                )
            part[g, 2 + zh, band(3), :] = whole(g, zh, 3)

    lower = core == 0

    def fold(v):
        return jnp.concatenate([v[0], v[1]], axis=0)

    def unfold(v):
        return [v[:TOP], v[TOP:]]

    home = None
    for zh in range(2):
        value = []
        for g in both:
            v = part[g, 2 + zh, band(3), :]
            drain(recv_q.at[g, zh, 0 : 3 * PIECE, :], across_sems.at[g * 2 + zh])
            for qs in range(RING - 1):
                v = v + recv_q[g, zh, band(qs), :].astype(F32)
            value.append(v)
        for j in range(4):
            k = (zh * 4 + j + 3) % DEPTH
            low = fold([v[j * ROWS : j * ROWS + TOP, :] for v in value])
            high = fold([v[j * ROWS + TOP : (j + 1) * ROWS, :] for v in value])
            for c, v in ((0, jnp.where(lower, low, high)), (1, jnp.where(lower, high, low))):
                if k + c == 0:
                    home = v
                    continue
                send_z[2 * k + c] = v.astype(BF16)
                send(send_z.at[2 * k + c], recv_z.at[(DEPTH - k) % DEPTH * 2 + c], line[k, c], 5, line_sems.at[0])
    fill(6, 10)
    got_old.wait_recv()
    drain(recv_z.at[1:], line_sems.at[0])
    other = recv_z[1].astype(F32)
    for k in range(1, DEPTH):
        home = home + recv_z[2 * k].astype(F32)
        other = other + recv_z[2 * k + 1].astype(F32)
    held = core == r

    def stale(side):
        return fold(
            [jnp.where(held, prod[my_rows, columns_of(side, g)], old_sib[:, columns_of(side, g)]) for g in both]
        )

    home = home + stale(core)
    other = other + stale(swap)
    squares = jnp.sum(home * home + other * other, axis=1, keepdims=True)
    scale = lax.rsqrt((squares[:TOP] + squares[TOP:]) * (1.0 / (2 * half)) + 1e-6)
    scale = fold([scale, scale])
    fresh = (home * scale).astype(BF16)
    send_g[0] = fresh
    send_g[1] = (other * scale).astype(BF16)
    recv_g[0] = fresh

    for k in (4, 3, 5, 2, 6, 1, 7, 0):
        for c in range(2):
            if k + c:
                zh = (HOME - k) % DEPTH // 4
                send(send_g.at[c], recv_g.at[(DEPTH - k) % DEPTH * 2 + c], line[k, c], 6, line_sems.at[1 + zh])
    fill(10, 16)

    def piece(ref, g, relp, zh, qs):
        start = spot(relp, zh, qs)
        return ref.at[g, start : start + PIECE, :]

    across, from_left, from_right = {}, {}, {}

    def share(g, relp, zh, qs):
        send(piece(tab, g, relp, zh, qs), piece(tab_sib, g, relp, zh, qs), sibling, 7, share_sems.at[relp])

    def first_ring(g, zh, qs):
        n = (g * 2 + zh) * RING + qs
        source = piece(tab, g, 0, zh, qs)
        from_left[g, zh, qs] = send(source, piece(tab, g, 3, zh, qs), right[g], 8, gather_sems.at[n])
        from_right[g, zh, qs] = send(source, piece(tab, g, 1, zh, qs), left[g], 8, gather_sems.at[16 + n])

    def pass_on(g, zh, qs):
        goes_right = (zh + qs) % 2 == 0
        for arrived, relp, to in ((from_left, 3, right), (from_right, 1, left)):
            arrived[g, zh, qs].wait_recv()
            if (relp == 3) == goes_right:
                send(piece(tab, g, relp, zh, qs), piece(tab, g, 2, zh, qs), to[g], 9, pass_sems.at[zh])
            share(g, relp, zh, qs)

    for zh in (1, 0):
        drain(recv_g.at[0 : 8 - zh], line_sems.at[1 + zh])
        for j in range(4):
            k = (zh * 4 + j + 3) % DEPTH
            same, sister = unfold(recv_g[2 * k].astype(F32)), unfold(recv_g[2 * k + 1].astype(F32))
            start = spot(0, zh, 3) + j * ROWS
            for g in both:
                upper, under = jnp.where(lower, same[g], sister[g]), jnp.where(lower, sister[g], same[g])
                tab[g, start : start + ROWS, :] = fold([upper, under]).astype(BF16)
        for d in (2, 1, 3):
            for g in both:
                n = (g * 2 + zh) * 3 + d - 1
                across[g, zh, d] = send(
                    piece(tab, g, 0, zh, 3), piece(tab, g, 0, zh, d - 1), around[g][d], 10, across_sems.at[4 + n]
                )
        for g in both:
            first_ring(g, zh, 3)
    for zh in (1, 0):
        for d in (1, 3, 2):
            for g in both:
                across[g, zh, d].wait_recv()
                first_ring(g, zh, d - 1)
        for g in both:
            pass_on(g, zh, 3)
    for zh in (1, 0):
        for qs in (3, 0, 2, 1):
            for g in both:
                share(g, 0, zh, qs)

    step = 256

    def picked(g, whiches, table, tok, relps):
        found = [
            jnp.dot(
                whiches[g][tok, relp * PB : (relp + 1) * PB], table[g, relp * PB : (relp + 1) * PB, :],
                preferred_element_type=F32,
            )
            for relp in relps
        ]
        return sum(found[1:], found[0])

    def look(state, whiches, table, relps):
        def tile(t, carry):
            tok = pl.ds(pl.multiple_of(t * step, step), step)
            for g in both:
                cols = slice(g * quarter, (g + 1) * quarter)
                rest = state[tok, cols].astype(F32) - picked(g, whiches, table, tok, relps)
                state[tok, cols] = rest.astype(BF16)
            return carry

        lax.fori_loop(0, tokens // step, tile, 0)

    hots, hots_sib = (hot, hot_sib), (hot_sib, hot)
    look(own, hots, tab, [0])
    loads[4].wait()
    drain(tab.at[:, 0:PB, :], share_sems.at[0])
    look(oth, hots_sib, tab_sib, [0])
    for zh in (1, 0):
        for qs in (0, 2, 1):
            for g in both:
                pass_on(g, zh, qs)
    look(own, hots, tab, [1, 3])
    drain(asg, send_sems.at[0])
    drain(own, send_sems.at[1])
    drain(send_p, send_sems.at[2])
    drain(old_sib, send_sems.at[3])
    drain(send_q.at[:, :, 0 : 3 * PIECE, :], send_sems.at[4])
    drain(send_z.at[1:], send_sems.at[5])
    drain(send_z.at[1:], send_sems.at[6])
    drain(tab.at[:, 0 : 2 * PB, :], send_sems.at[8])
    drain(tab.at[:, 0 : 6 * PIECE, :], send_sems.at[10])
    drain(tab.at[:, 0:PB, :], share_sems.at[1])
    drain(tab.at[:, 0:PB, :], share_sems.at[3])
    look(oth, hots_sib, tab_sib, [1, 3])
    last = []
    for zh in (1, 0):
        drain(tab.at[:, 0:HALF, :], pass_sems.at[zh])
        there = slice(spot(2, zh, 0), spot(2, zh, 0) + HALF)
        last.append(send(tab.at[:, there, :], tab_sib.at[:, there, :], sibling, 11 + zh, pass_sems.at[2 + zh]))

    def finish(state, whiches, table, side):
        def tile(t, carry):
            tok = pl.ds(pl.multiple_of(t * step, step), step)
            for g in both:
                rest = state[tok, g * quarter : (g + 1) * quarter].astype(F32)
                out[tok, columns_of(side, g)] = (rest - picked(g, whiches, table, tok, [2])).astype(BF16)
            return carry

        lax.fori_loop(0, tokens // step, tile, 0)

    finish(own, hots, tab, core)
    for copy in last:
        copy.wait_recv()
    finish(oth, hots_sib, tab_sib, swap)

    away = lax.rem(core + r, 2) * 2
    base = HALF + (HOME - 4) * ROWS

    def spot_of(turn):
        start = base + (1 - turn) * (3 - away) * PIECE + turn * (away * PB + 3 * PIECE)
        return pl.ds(pl.multiple_of(start, ROWS), ROWS)

    for g in both:
        new_out[:, columns_of(core, g)] = tab[g, spot_of(turns[g]), :]
        new_out[:, columns_of(swap, g)] = tab_sib[g, spot_of(turns[1 - g]), :]
    drain(tab.at[:, 0 : 3 * PB, :], send_sems.at[7])
    drain(tab.at[:, 0:PB, :], send_sems.at[9])
    for copy in last:
        copy.wait_send()


def body(embeddings, assignments, old_centroids, old_counts):
    tokens, width = embeddings.shape
    half, table = width // 2, RING * PB
    vmem, dma = pltpu.VMEM, pltpu.SemaphoreType.DMA
    operands = (embeddings, assignments.reshape(1, tokens), old_centroids, old_counts.reshape(1, ROWS))
    hbm = pl.BlockSpec(memory_space=pltpu.HBM)
    return pl.pallas_call(
        kernel,
        out_shape=(vmem((tokens, width), BF16), vmem((ROWS, width), BF16)),
        in_specs=[hbm] * 4,
        out_specs=(pl.BlockSpec(memory_space=vmem), pl.BlockSpec(memory_space=vmem)),
        scratch_shapes=[
            vmem((tokens, half), BF16),
            vmem((tokens, half), BF16),
            vmem((tokens, half), BF16),
            vmem((1, tokens), I32),
            vmem((1, tokens), I32),
            vmem((ROWS, width), BF16),
            vmem((1, ROWS), I32),
            vmem((ROWS, width), F32),
            vmem((TOP, width), F32),
            vmem((2, PB, 128), I16),
            vmem((HALF, 2 * tokens), BF16),
            vmem((2, 6, HALF, half // 2), BF16),
            vmem((2, 6, HALF, half // 2), BF16),
            vmem((2, 4, HALF, half // 2), F32),
            vmem((2, 2, HALF, half // 2), BF16),
            vmem((2, 2, HALF, half // 2), BF16),
            vmem((2 * DEPTH, ROWS, half // 2), BF16),
            vmem((2 * DEPTH, ROWS, half // 2), BF16),
            vmem((2, ROWS, half // 2), BF16),
            vmem((2 * DEPTH, ROWS, half // 2), BF16),
            vmem((2, table, half // 2), BF16),
            vmem((2, table, half // 2), BF16),
            vmem((tokens, 128), I16),
            vmem((tokens, table), BF16),
            vmem((tokens, table), BF16),
            dma((5,)),
            dma((13,)),
            dma((3,)),
            dma((16,)),
            dma((4,)),
            dma((16,)),
            dma((16,)),
            dma((3,)),
            dma((32,)),
            dma((4,)),
            dma((4,)),
        ],
        compiler_params=pltpu.CompilerParams(
            collective_id=0, has_side_effects=True, vmem_limit_bytes=58 * 1024 * 1024
        ),
        cost_estimate=pl.CostEstimate(flops=8 * 2**30, bytes_accessed=4 * 2**20, transcendentals=0),
    )(*[pltpu.with_memory_space_constraint(operand, pltpu.HBM) for operand in operands])


def solution(mesh):
    placed = (P(("corpus", "rep"), None), P(("corpus", "rep")), P("corpus", None), P("corpus"))
    return jax.shard_map(
        body,
        mesh=mesh,
        in_specs=placed,
        out_specs=(P(("corpus", "rep"), None), P("corpus", None)),
        check_vma=False,
    )
```

```python
import jax
import jax.numpy as jnp
from jax import lax
from jax.experimental import pallas as pl
from jax.experimental.pallas import tpu as pltpu
from jax.sharding import PartitionSpec as P

MESH = pl.DeviceIdType.MESH
F32, BF16, I32, I16 = jnp.float32, jnp.bfloat16, jnp.int32, jnp.int16

RING, DEPTH, ROWS = 4, 8, 16
PIECE = DEPTH // 2 * ROWS
HALF = RING * PIECE
PB = 2 * HALF
HOME = 5
TOP = ROWS // 2


def place():
    c, r = lax.axis_index("corpus"), lax.axis_index("rep")
    core, x, z, ylo = c % 2, (c // 2) % RING, (c // (2 * RING)) % DEPTH, c // (2 * RING * DEPTH)
    return core, x, r * 2 + ylo, z, r


def device(core, x, y, z):
    return (((y % 2) * DEPTH + z) * RING + x) * 2 + core, y // 2


def label_of(i, core, x, y, z):
    p0, q0 = x + core * (y - x), y + core * (x - y)
    p = (p0 + (i >> 9)) & 3
    q = (q0 + 3 - ((i >> 6) & 3)) & 3
    zz = (z + 3 + ((i >> 4) & 3) + ((i >> 6) & 4)) & 7
    xx, yy = p + core * (q - p), q + core * (p - q)
    return (((((yy & 1) * DEPTH + zz) * RING + xx) * 2 + (yy >> 1)) << 4) + (i & 15)


def label_parts(i, core, x, y, z):
    q = ((y + core * (x - y)) + 3 - ((i >> 6) & 3)) & 3
    zz = (z + 3 + ((i >> 4) & 3) + ((i >> 6) & 4)) & 7
    first = ((((q & 1) * DEPTH + zz) * RING * 2 + (q >> 1)) << 4) + (i & 15)
    second = (((zz * RING + q) * 2) << 4) + (i & 15)
    return first + core * (second - first)


def shift_of(p, core):
    first = p * 2 * ROWS
    second = (p % 2) * (DEPTH * RING * 2 * ROWS) + (p // 2) * ROWS
    return first + core * (second - first)


def spot(relp, zh, qs):
    return relp * PB + zh * HALF + qs * PIECE


def kernel(
    emb, asg_in, old_in, cnt_in, out, new_out,
    own, sib, oth, asg, asg_sib, old, cnt, prod, old_sib,
    labels, hot_p, send_p, recv_p, part, send_q, recv_q, send_z, recv_z, send_g, recv_g,
    tab, tab_sib, asg_t, hot, hot_sib,
    load_sems, send_sems, swap_sems, near_sems, far_sems, ring_sems, across_sems, line_sems,
    gather_sems, pass_sems, share_sems,
):
    core, x, y, z, r = place()
    tokens, half = own.shape
    swap = 1 - core
    p0, q0 = x + core * (y - x), y + core * (x - y)

    def pq(p, q):
        p, q = lax.rem(p, RING), lax.rem(q, RING)
        return device(core, p + core * (q - p), q + core * (p - q), z)

    sibling = device(swap, x, y, z)
    right, left = pq(p0 + 1, q0), pq(p0 + 3, q0)
    around = [None] + [pq(p0, q0 + d) for d in range(1, RING)]
    line = {
        (k, c): device(swap if c else core, x, y, lax.rem(z + k, DEPTH))
        for k in range(DEPTH) for c in range(2) if k + c
    }

    barrier = pltpu.get_barrier_semaphore()
    everyone = [right, left] + around[1:] + [line[key] for key in line]
    for other in everyone:
        pl.semaphore_signal(barrier, inc=1, device_id=other, device_id_type=MESH)

    mine = pl.ds(pl.multiple_of(core * half, 128), half)
    theirs = pl.ds(pl.multiple_of(swap * half, 128), half)
    loads = [
        pltpu.make_async_copy(a, b, load_sems.at[n])
        for n, (a, b) in enumerate(
            [(asg_in, asg), (emb.at[:, mine], own), (old_in, old), (cnt_in, cnt), (emb.at[:, theirs], oth)]
        )
    ]
    for load in loads:
        load.start()

    def send(src, dst, to, group, sem):
        copy = pltpu.make_async_remote_copy(
            src_ref=src, dst_ref=dst, send_sem=send_sems.at[group], recv_sem=sem,
            device_id=to, device_id_type=MESH,
        )
        copy.start()
        return copy

    def drain(ref, sem):
        pltpu.make_async_copy(ref, ref, sem).wait()

    pl.semaphore_wait(barrier, len(everyone))
    got_asg = send(asg_in, asg_sib, sibling, 0, swap_sems.at[0])
    tk = tokens // 2
    got_emb = [
        send(emb.at[n * tk : (n + 1) * tk, theirs], sib.at[n * tk : (n + 1) * tk, :], sibling, 1, swap_sems.at[1 + 2 * n])
        for n in range(2)
    ]

    i = lax.broadcasted_iota(I32, (PB, 128), 0)
    labels[...] = label_parts(i, core, x, y, z).astype(I16)
    loads[0].wait()
    loads[1].wait()
    one, zero = jnp.bfloat16(1), jnp.bfloat16(0)

    def chunk(relp, zh, first=False):
        shift = shift_of(lax.rem(p0 + relp, RING), core)
        wanted = labels[zh * HALF : (zh + 1) * HALF, :]

        def hot_rows(ids, base):
            moved = (ids[...] - shift).astype(I16)
            for t in range(0, tokens, 128):
                hot_p[:, base + t : base + t + 128] = jnp.where(wanted == moved[:, t : t + 128], one, zero)

        hot_rows(asg, 0)
        total = jnp.dot(hot_p[:, 0:tokens], own[...], preferred_element_type=F32)
        if first:
            got_asg.wait_recv()
        hot_rows(asg_sib, tokens)
        if first:
            for n in range(2):
                got_emb[n].wait_recv()
                there = hot_p[:, tokens + n * tk : tokens + (n + 1) * tk]
                total = total + jnp.dot(there, sib[n * tk : (n + 1) * tk, :], preferred_element_type=F32)
            return total
        return total + jnp.dot(hot_p[:, tokens : 2 * tokens], sib[...], preferred_element_type=F32)

    def band(qs):
        return slice(qs * PIECE, (qs + 1) * PIECE)

    def ring(n, to, qs, sem):
        return send(send_p.at[n, band(qs), :], recv_p.at[n, band(qs), :], to, 2, sem)

    send_p[0] = chunk(2, 0, True).astype(BF16)
    r1 = [ring(0, right, qs, near_sems.at[qs]) for qs in range(RING)]
    send_p[1] = chunk(2, 1).astype(BF16)
    l1 = [ring(1, left, qs, near_sems.at[RING + qs]) for qs in range(RING)]
    send_p[2] = chunk(1, 1).astype(BF16)
    for qs in range(RING):
        ring(2, right, qs, far_sems.at[0])
    send_p[3] = chunk(3, 0).astype(BF16)
    for qs in range(RING):
        ring(3, left, qs, far_sems.at[1])
    part[0] = chunk(1, 0)
    part[1] = chunk(3, 1)
    r3, l3 = [], []
    for copies, arrived, n, to in ((r3, r1, 0, right), (l3, l1, 1, left)):
        for qs in range(RING):
            arrived[qs].wait_recv()
            send_p[4 + n, band(qs), :] = (part[n, band(qs), :] + recv_p[n, band(qs), :].astype(F32)).astype(BF16)
            copies.append(ring(4 + n, to, qs, ring_sems.at[n * RING + qs]))
    part[2] = chunk(0, 0)
    part[3] = chunk(0, 1)

    loads[2].wait()
    loads[3].wait()
    eye = lax.broadcasted_iota(I32, (ROWS, ROWS), 0) == lax.broadcasted_iota(I32, (ROWS, ROWS), 1)
    weight = jnp.sum(jnp.where(eye, cnt[...].astype(F32), 0.0), axis=1, keepdims=True)
    prod[...] = weight * old[...].astype(F32)
    my_rows = pl.ds(pl.multiple_of(core * TOP, TOP), TOP)
    their_rows = pl.ds(pl.multiple_of(swap * TOP, TOP), TOP)
    got_old = send(prod.at[their_rows, :], old_sib, sibling, 3, swap_sems.at[2])

    for t in range(0, tokens, 128):
        row = jnp.broadcast_to(asg[:, t : t + 128], (128, 128))
        asg_t[t : t + 128, :] = row.T.astype(I16)

    def fill(low, high):
        def lanes_of(b, carry):
            i = lax.broadcasted_iota(I32, (ROWS, 128), 1) + b * 128
            lanes = pl.ds(pl.multiple_of(b * 128, 128), 128)
            for ref, which in ((hot, core), (hot_sib, swap)):
                row = label_of(i, which, x, y, z).astype(I16)
                ref[:, lanes] = jnp.where(asg_t[...] == row[0:1, :], one, zero)
            return carry

        lax.fori_loop(low, high, lanes_of, 0)

    fill(0, 8)

    drain(recv_p.at[2], far_sems.at[0])
    drain(recv_p.at[3], far_sems.at[1])

    def whole(zh, qs):
        (r3, l3)[zh][qs].wait_recv()
        m, n = (4, 3) if zh == 0 else (5, 2)
        return part[2 + zh, band(qs), :] + (recv_p[m, band(qs), :].astype(F32) + recv_p[n, band(qs), :].astype(F32))

    for zh in range(2):
        for qs in range(RING - 1):
            send_q[zh, band(qs), :] = whole(zh, qs).astype(BF16)
            send(send_q.at[zh, band(qs), :], recv_q.at[zh, band(qs), :], around[3 - qs], 4, across_sems.at[zh])
        part[2 + zh, band(3), :] = whole(zh, 3)

    lower = core == 0

    def fold(v):
        return jnp.concatenate([v[:, : half // 2], v[:, half // 2 :]], axis=0)

    def unfold(v):
        return jnp.concatenate([v[:TOP], v[TOP:]], axis=1)

    home = None
    for zh in range(2):
        value = part[2 + zh, band(3), :]
        drain(recv_q.at[zh, 0 : 3 * PIECE, :], across_sems.at[zh])
        for qs in range(RING - 1):
            value = value + recv_q[zh, band(qs), :].astype(F32)
        for j in range(4):
            k = (zh * 4 + j + 3) % DEPTH
            low, high = value[j * ROWS : j * ROWS + TOP, :], value[j * ROWS + TOP : (j + 1) * ROWS, :]
            for c, v in ((0, jnp.where(lower, low, high)), (1, jnp.where(lower, high, low))):
                if k + c == 0:
                    home = fold(v)
                    continue
                send_z[2 * k + c] = fold(v).astype(BF16)
                send(send_z.at[2 * k + c], recv_z.at[(DEPTH - k) % DEPTH * 2 + c], line[k, c], 5, line_sems.at[0])
    fill(8, 11)
    got_old.wait_recv()
    drain(recv_z.at[1:], line_sems.at[0])
    other = recv_z[1].astype(F32)
    for k in range(1, DEPTH):
        home = home + recv_z[2 * k].astype(F32)
        other = other + recv_z[2 * k + 1].astype(F32)
    held = core == r
    home = unfold(home) + jnp.where(held, prod[my_rows, mine], old_sib[:, mine])
    other = unfold(other) + jnp.where(held, prod[my_rows, theirs], old_sib[:, theirs])
    squares = jnp.sum(home * home, axis=1, keepdims=True) + jnp.sum(other * other, axis=1, keepdims=True)
    scale = lax.rsqrt(squares * (1.0 / (2 * half)) + 1e-6)
    fresh = fold(home * scale).astype(BF16)
    send_g[0] = fresh
    send_g[1] = fold(other * scale).astype(BF16)
    recv_g[0] = fresh

    for k in (4, 3, 5, 2, 6, 1, 7, 0):
        for c in range(2):
            if k + c:
                zh = (HOME - k) % DEPTH // 4
                send(send_g.at[c], recv_g.at[(DEPTH - k) % DEPTH * 2 + c], line[k, c], 6, line_sems.at[1 + zh])
    fill(11, 16)

    def piece(ref, relp, zh, qs):
        start = spot(relp, zh, qs)
        return ref.at[start : start + PIECE, :]

    across, from_left, from_right = {}, {}, {}

    def share(relp, zh, qs):
        send(piece(tab, relp, zh, qs), piece(tab_sib, relp, zh, qs), sibling, 7, share_sems.at[relp])

    def first_ring(zh, qs):
        n = zh * RING + qs
        from_left[zh, qs] = send(piece(tab, 0, zh, qs), piece(tab, 3, zh, qs), right, 8, gather_sems.at[n])
        from_right[zh, qs] = send(piece(tab, 0, zh, qs), piece(tab, 1, zh, qs), left, 8, gather_sems.at[8 + n])
        share(0, zh, qs)

    def pass_on(zh, qs):
        goes_right = (zh + qs) % 2 == 0
        for arrived, relp, to in ((from_left, 3, right), (from_right, 1, left)):
            arrived[zh, qs].wait_recv()
            if (relp == 3) == goes_right:
                send(piece(tab, relp, zh, qs), piece(tab, 2, zh, qs), to, 9, pass_sems.at[zh])
            share(relp, zh, qs)

    for zh in (1, 0):
        drain(recv_g.at[0 : 8 - zh], line_sems.at[1 + zh])
        for j in range(4):
            k = (zh * 4 + j + 3) % DEPTH
            same, sister = unfold(recv_g[2 * k].astype(F32)), unfold(recv_g[2 * k + 1].astype(F32))
            block = jnp.concatenate([jnp.where(lower, same, sister), jnp.where(lower, sister, same)], axis=0)
            start = spot(0, zh, 3) + j * ROWS
            tab[start : start + ROWS, :] = block.astype(BF16)
        for d in (2, 1, 3):
            n = zh * 3 + d - 1
            across[zh, d] = send(
                piece(tab, 0, zh, 3), piece(tab, 0, zh, d - 1), around[d], 10, across_sems.at[2 + n]
            )
        first_ring(zh, 3)
    for zh in (1, 0):
        for d in (1, 3, 2):
            across[zh, d].wait_recv()
            first_ring(zh, d - 1)
        pass_on(zh, 3)

    step = 512

    def look(state, which, table, spans):
        def tile(t, carry):
            tok = pl.ds(pl.multiple_of(t * step, step), step)
            picked = [
                jnp.dot(which[tok, a : a + n], table[a : a + n, :], preferred_element_type=F32) for a, n in spans
            ]
            state[tok, :] = (state[tok, :].astype(F32) - sum(picked[1:], picked[0])).astype(BF16)
            return carry

        lax.fori_loop(0, tokens // step, tile, 0)

    look(own, hot, tab, [(0, PB)])
    loads[4].wait()
    drain(tab.at[0:PB, :], share_sems.at[0])
    look(oth, hot_sib, tab_sib, [(0, PB)])
    for qs in (0, 2, 1):
        pass_on(1, qs)
    look(own, hot, tab, [(PB + HALF, HALF), (3 * PB + HALF, HALF)])
    for qs in (0, 2, 1):
        pass_on(0, qs)
    look(own, hot, tab, [(PB, HALF), (3 * PB, HALF)])
    last = []

    def hand_over(zh):
        drain(tab.at[0:HALF, :], pass_sems.at[zh])
        start = spot(2, zh, 0)
        last.append(
            send(tab.at[start : start + HALF, :], tab_sib.at[start : start + HALF, :], sibling, 11 + zh, pass_sems.at[2 + zh])
        )

    drain(tab.at[0:PB, :], share_sems.at[1])
    drain(tab.at[0:PB, :], share_sems.at[3])
    hand_over(1)
    look(oth, hot_sib, tab_sib, [(PB, PB), (3 * PB, PB)])
    hand_over(0)
    drain(asg, send_sems.at[0])
    drain(own, send_sems.at[1])
    drain(send_p, send_sems.at[2])
    drain(old_sib, send_sems.at[3])
    drain(send_q.at[:, 0 : 3 * PIECE, :], send_sems.at[4])
    drain(send_z.at[1:], send_sems.at[5])
    drain(send_z.at[1:], send_sems.at[6])
    drain(tab.at[0 : 2 * PB, :], send_sems.at[8])
    drain(tab.at[0 : 6 * PIECE, :], send_sems.at[10])

    def finish(state, which, table, columns):
        def tile(t, carry):
            tok = pl.ds(pl.multiple_of(t * step, step), step)
            picked = jnp.dot(which[tok, 2 * PB : 3 * PB], table[2 * PB : 3 * PB, :], preferred_element_type=F32)
            out[tok, columns] = (state[tok, :].astype(F32) - picked).astype(BF16)
            return carry

        lax.fori_loop(0, tokens // step, tile, 0)

    finish(own, hot, tab, mine)
    for copy in last:
        copy.wait_recv()
    finish(oth, hot_sib, tab_sib, theirs)

    away = lax.rem(core + r, 2) * 2
    base = HALF + (HOME - 4) * ROWS
    a = base + swap * (3 - away) * PIECE + core * (away * PB + 3 * PIECE)
    b = base + core * (3 - away) * PIECE + swap * (away * PB + 3 * PIECE)
    new_out[:, mine] = tab[pl.ds(pl.multiple_of(a, ROWS), ROWS), :]
    new_out[:, theirs] = tab_sib[pl.ds(pl.multiple_of(b, ROWS), ROWS), :]
    drain(tab.at[0 : 3 * PB, :], send_sems.at[7])
    drain(tab.at[0:PB, :], send_sems.at[9])
    for copy in last:
        copy.wait_send()


def body(embeddings, assignments, old_centroids, old_counts):
    tokens, width = embeddings.shape
    half, table = width // 2, RING * PB
    vmem, dma = pltpu.VMEM, pltpu.SemaphoreType.DMA
    operands = (embeddings, assignments.reshape(1, tokens), old_centroids, old_counts.reshape(1, ROWS))
    hbm = pl.BlockSpec(memory_space=pltpu.HBM)
    return pl.pallas_call(
        kernel,
        out_shape=(vmem((tokens, width), BF16), vmem((ROWS, width), BF16)),
        in_specs=[hbm] * 4,
        out_specs=(pl.BlockSpec(memory_space=vmem), pl.BlockSpec(memory_space=vmem)),
        scratch_shapes=[
            vmem((tokens, half), BF16),
            vmem((tokens, half), BF16),
            vmem((tokens, half), BF16),
            vmem((1, tokens), I32),
            vmem((1, tokens), I32),
            vmem((ROWS, width), BF16),
            vmem((1, ROWS), I32),
            vmem((ROWS, width), F32),
            vmem((TOP, width), F32),
            vmem((PB, 128), I16),
            vmem((HALF, 2 * tokens), BF16),
            vmem((6, HALF, half), BF16),
            vmem((6, HALF, half), BF16),
            vmem((4, HALF, half), F32),
            vmem((2, HALF, half), BF16),
            vmem((2, HALF, half), BF16),
            vmem((2 * DEPTH, ROWS, half // 2), BF16),
            vmem((2 * DEPTH, ROWS, half // 2), BF16),
            vmem((2, ROWS, half // 2), BF16),
            vmem((2 * DEPTH, ROWS, half // 2), BF16),
            vmem((table, half), BF16),
            vmem((table, half), BF16),
            vmem((tokens, 128), I16),
            vmem((tokens, table), BF16),
            vmem((tokens, table), BF16),
            dma((5,)),
            dma((13,)),
            dma((4,)),
            dma((8,)),
            dma((2,)),
            dma((8,)),
            dma((8,)),
            dma((3,)),
            dma((16,)),
            dma((4,)),
            dma((4,)),
        ],
        compiler_params=pltpu.CompilerParams(
            collective_id=0, has_side_effects=True, vmem_limit_bytes=58 * 1024 * 1024
        ),
        cost_estimate=pl.CostEstimate(flops=8 * 2**30, bytes_accessed=4 * 2**20, transcendentals=0),
    )(*[pltpu.with_memory_space_constraint(operand, pltpu.HBM) for operand in operands])


def solution(mesh):
    placed = (P(("corpus", "rep"), None), P(("corpus", "rep")), P("corpus", None), P("corpus"))
    return jax.shard_map(
        body,
        mesh=mesh,
        in_specs=placed,
        out_specs=(P(("corpus", "rep"), None), P("corpus", None)),
        check_vma=False,
    )
```

```python
import jax
import jax.numpy as jnp
from jax import lax
from jax.experimental import pallas as pl
from jax.experimental.pallas import tpu as pltpu
from jax.sharding import PartitionSpec as P

MESH = pl.DeviceIdType.MESH
F32, BF16, I32, I16 = jnp.float32, jnp.bfloat16, jnp.int32, jnp.int16

RING, DEPTH, ROWS = 4, 8, 16
PIECE = DEPTH // 2 * ROWS
HALF = RING * PIECE
PB = 2 * HALF
HOME = 5
TOP = ROWS // 2


def place():
    c, r = lax.axis_index("corpus"), lax.axis_index("rep")
    core, x, z, ylo = c % 2, (c // 2) % RING, (c // (2 * RING)) % DEPTH, c // (2 * RING * DEPTH)
    return core, x, r * 2 + ylo, z, r


def device(core, x, y, z):
    return (((y % 2) * DEPTH + z) * RING + x) * 2 + core, y // 2


def label_of(i, core, x, y, z):
    p0, q0 = x + core * (y - x), y + core * (x - y)
    p = (p0 + (i >> 9)) & 3
    q = (q0 + 3 - ((i >> 6) & 3)) & 3
    zz = (z + 3 + ((i >> 4) & 3) + ((i >> 6) & 4)) & 7
    xx, yy = p + core * (q - p), q + core * (p - q)
    return (((((yy & 1) * DEPTH + zz) * RING + xx) * 2 + (yy >> 1)) << 4) + (i & 15)


def label_parts(i, core, x, y, z):
    q = ((y + core * (x - y)) + 3 - ((i >> 6) & 3)) & 3
    zz = (z + 3 + ((i >> 4) & 3) + ((i >> 6) & 4)) & 7
    first = ((((q & 1) * DEPTH + zz) * RING * 2 + (q >> 1)) << 4) + (i & 15)
    second = (((zz * RING + q) * 2) << 4) + (i & 15)
    return first + core * (second - first)


def shift_of(p, core):
    first = p * 2 * ROWS
    second = (p % 2) * (DEPTH * RING * 2 * ROWS) + (p // 2) * ROWS
    return first + core * (second - first)


def spot(relp, zh, qs):
    return relp * PB + zh * HALF + qs * PIECE


def kernel(
    emb, asg_in, old_in, cnt_in, out, new_out,
    own, sib, oth, asg, asg_sib, old, cnt, prod, old_sib,
    labels, hot_p, send_p, recv_p, part, send_q, recv_q, send_z, recv_z, send_g, recv_g,
    tab, tab_sib, asg_t, hot, hot_sib,
    load_sems, send_sems, swap_sems, near_sems, far_sems, ring_sems, across_sems, line_sems,
    gather_sems, pass_sems, share_sems,
):
    core, x, y, z, r = place()
    tokens, half = own.shape
    swap = 1 - core
    p0, q0 = x + core * (y - x), y + core * (x - y)

    def pq(p, q):
        p, q = lax.rem(p, RING), lax.rem(q, RING)
        return device(core, p + core * (q - p), q + core * (p - q), z)

    sibling = device(swap, x, y, z)
    right, left = pq(p0 + 1, q0), pq(p0 + 3, q0)
    around = [None] + [pq(p0, q0 + d) for d in range(1, RING)]
    line = {
        (k, c): device(swap if c else core, x, y, lax.rem(z + k, DEPTH))
        for k in range(DEPTH) for c in range(2) if k + c
    }

    barrier = pltpu.get_barrier_semaphore()
    everyone = [right, left] + around[1:] + [line[key] for key in line]
    for other in everyone:
        pl.semaphore_signal(barrier, inc=1, device_id=other, device_id_type=MESH)

    mine = pl.ds(pl.multiple_of(core * half, 128), half)
    theirs = pl.ds(pl.multiple_of(swap * half, 128), half)
    loads = [
        pltpu.make_async_copy(a, b, load_sems.at[n])
        for n, (a, b) in enumerate(
            [(asg_in, asg), (emb.at[:, mine], own), (old_in, old), (cnt_in, cnt), (emb.at[:, theirs], oth)]
        )
    ]
    for load in loads:
        load.start()

    def send(src, dst, to, group, sem):
        copy = pltpu.make_async_remote_copy(
            src_ref=src, dst_ref=dst, send_sem=send_sems.at[group], recv_sem=sem,
            device_id=to, device_id_type=MESH,
        )
        copy.start()
        return copy

    def drain(ref, sem):
        pltpu.make_async_copy(ref, ref, sem).wait()

    pl.semaphore_wait(barrier, len(everyone))
    got_asg = send(asg_in, asg_sib, sibling, 0, swap_sems.at[0])
    tk = tokens // 2
    got_emb = [
        send(emb.at[n * tk : (n + 1) * tk, theirs], sib.at[n * tk : (n + 1) * tk, :], sibling, 1, swap_sems.at[1 + 2 * n])
        for n in range(2)
    ]

    i = lax.broadcasted_iota(I32, (PB, 128), 0)
    labels[...] = label_parts(i, core, x, y, z).astype(I16)
    loads[0].wait()
    loads[1].wait()
    one, zero = jnp.bfloat16(1), jnp.bfloat16(0)

    def chunk(relp, zh, first=False):
        shift = shift_of(lax.rem(p0 + relp, RING), core)
        wanted = labels[zh * HALF : (zh + 1) * HALF, :]

        def hot_rows(ids, base):
            moved = (ids[...] - shift).astype(I16)
            for t in range(0, tokens, 128):
                hot_p[:, base + t : base + t + 128] = jnp.where(wanted == moved[:, t : t + 128], one, zero)

        hot_rows(asg, 0)
        total = jnp.dot(hot_p[:, 0:tokens], own[...], preferred_element_type=F32)
        if first:
            got_asg.wait_recv()
        hot_rows(asg_sib, tokens)
        if first:
            for n in range(2):
                got_emb[n].wait_recv()
                there = hot_p[:, tokens + n * tk : tokens + (n + 1) * tk]
                total = total + jnp.dot(there, sib[n * tk : (n + 1) * tk, :], preferred_element_type=F32)
            return total
        return total + jnp.dot(hot_p[:, tokens : 2 * tokens], sib[...], preferred_element_type=F32)

    def band(qs):
        return slice(qs * PIECE, (qs + 1) * PIECE)

    def ring(n, to, qs, sem):
        return send(send_p.at[n, band(qs), :], recv_p.at[n, band(qs), :], to, 2, sem)

    send_p[0] = chunk(2, 0, True).astype(BF16)
    r1 = [ring(0, right, qs, near_sems.at[qs]) for qs in range(RING)]
    send_p[1] = chunk(2, 1).astype(BF16)
    l1 = [ring(1, left, qs, near_sems.at[RING + qs]) for qs in range(RING)]
    send_p[2] = chunk(1, 1).astype(BF16)
    for qs in range(RING):
        ring(2, right, qs, far_sems.at[0])
    send_p[3] = chunk(3, 0).astype(BF16)
    for qs in range(RING):
        ring(3, left, qs, far_sems.at[1])
    part[0] = chunk(1, 0)
    part[1] = chunk(3, 1)
    r3, l3 = [], []
    for copies, arrived, n, to in ((r3, r1, 0, right), (l3, l1, 1, left)):
        for qs in range(RING):
            arrived[qs].wait_recv()
            send_p[4 + n, band(qs), :] = (part[n, band(qs), :] + recv_p[n, band(qs), :].astype(F32)).astype(BF16)
            copies.append(ring(4 + n, to, qs, ring_sems.at[n * RING + qs]))
    part[2] = chunk(0, 0)
    part[3] = chunk(0, 1)

    loads[2].wait()
    loads[3].wait()
    eye = lax.broadcasted_iota(I32, (ROWS, ROWS), 0) == lax.broadcasted_iota(I32, (ROWS, ROWS), 1)
    weight = jnp.sum(jnp.where(eye, cnt[...].astype(F32), 0.0), axis=1, keepdims=True)
    prod[...] = weight * old[...].astype(F32)
    my_rows = pl.ds(pl.multiple_of(core * TOP, TOP), TOP)
    their_rows = pl.ds(pl.multiple_of(swap * TOP, TOP), TOP)
    got_old = send(prod.at[their_rows, :], old_sib, sibling, 3, swap_sems.at[2])

    for t in range(0, tokens, 128):
        row = jnp.broadcast_to(asg[:, t : t + 128], (128, 128))
        asg_t[t : t + 128, :] = row.T.astype(I16)

    def fill(low, high):
        def lanes_of(b, carry):
            i = lax.broadcasted_iota(I32, (ROWS, 128), 1) + b * 128
            lanes = pl.ds(pl.multiple_of(b * 128, 128), 128)
            for ref, which in ((hot, core), (hot_sib, swap)):
                row = label_of(i, which, x, y, z).astype(I16)
                ref[:, lanes] = jnp.where(asg_t[...] == row[0:1, :], one, zero)
            return carry

        lax.fori_loop(low, high, lanes_of, 0)

    fill(0, 8)

    drain(recv_p.at[2], far_sems.at[0])
    drain(recv_p.at[3], far_sems.at[1])

    def whole(zh, qs):
        (r3, l3)[zh][qs].wait_recv()
        m, n = (4, 3) if zh == 0 else (5, 2)
        return part[2 + zh, band(qs), :] + (recv_p[m, band(qs), :].astype(F32) + recv_p[n, band(qs), :].astype(F32))

    for zh in range(2):
        for qs in range(RING - 1):
            send_q[zh, band(qs), :] = whole(zh, qs).astype(BF16)
            send(send_q.at[zh, band(qs), :], recv_q.at[zh, band(qs), :], around[3 - qs], 4, across_sems.at[zh])
        part[2 + zh, band(3), :] = whole(zh, 3)

    lower = core == 0

    def fold(v):
        return jnp.concatenate([v[:, : half // 2], v[:, half // 2 :]], axis=0)

    def unfold(v):
        return jnp.concatenate([v[:TOP], v[TOP:]], axis=1)

    home = None
    for zh in range(2):
        value = part[2 + zh, band(3), :]
        drain(recv_q.at[zh, 0 : 3 * PIECE, :], across_sems.at[zh])
        for qs in range(RING - 1):
            value = value + recv_q[zh, band(qs), :].astype(F32)
        for j in range(4):
            k = (zh * 4 + j + 3) % DEPTH
            low, high = value[j * ROWS : j * ROWS + TOP, :], value[j * ROWS + TOP : (j + 1) * ROWS, :]
            for c, v in ((0, jnp.where(lower, low, high)), (1, jnp.where(lower, high, low))):
                if k + c == 0:
                    home = fold(v)
                    continue
                send_z[2 * k + c] = fold(v).astype(BF16)
                send(send_z.at[2 * k + c], recv_z.at[(DEPTH - k) % DEPTH * 2 + c], line[k, c], 5, line_sems.at[0])
    fill(8, 11)
    got_old.wait_recv()
    drain(recv_z.at[1:], line_sems.at[0])
    other = recv_z[1].astype(F32)
    for k in range(1, DEPTH):
        home = home + recv_z[2 * k].astype(F32)
        other = other + recv_z[2 * k + 1].astype(F32)
    held = core == r
    home = unfold(home) + jnp.where(held, prod[my_rows, mine], old_sib[:, mine])
    other = unfold(other) + jnp.where(held, prod[my_rows, theirs], old_sib[:, theirs])
    squares = jnp.sum(home * home, axis=1, keepdims=True) + jnp.sum(other * other, axis=1, keepdims=True)
    scale = lax.rsqrt(squares * (1.0 / (2 * half)) + 1e-6)
    fresh = fold(home * scale).astype(BF16)
    send_g[0] = fresh
    send_g[1] = fold(other * scale).astype(BF16)
    recv_g[0] = fresh

    for k in (1, 7, 6, 0, 4, 3, 5, 2):
        for c in range(2):
            if k + c:
                zh = (HOME - k) % DEPTH // 4
                send(send_g.at[c], recv_g.at[(DEPTH - k) % DEPTH * 2 + c], line[k, c], 6, line_sems.at[1 + zh])
    fill(11, 16)

    def piece(ref, relp, zh, qs):
        start = spot(relp, zh, qs)
        return ref.at[start : start + PIECE, :]

    across, from_left, from_right = {}, {}, {}

    def share(relp, zh, qs):
        send(piece(tab, relp, zh, qs), piece(tab_sib, relp, zh, qs), sibling, 7, share_sems.at[relp])

    def first_ring(zh, qs):
        n = zh * RING + qs
        from_left[zh, qs] = send(piece(tab, 0, zh, qs), piece(tab, 3, zh, qs), right, 8, gather_sems.at[n])
        from_right[zh, qs] = send(piece(tab, 0, zh, qs), piece(tab, 1, zh, qs), left, 8, gather_sems.at[8 + n])
        share(0, zh, qs)

    def pass_on(zh, qs):
        goes_right = (zh + qs) % 2 == 0
        for arrived, relp, to in ((from_left, 3, right), (from_right, 1, left)):
            arrived[zh, qs].wait_recv()
            if (relp == 3) == goes_right:
                send(piece(tab, relp, zh, qs), piece(tab, 2, zh, qs), to, 9, pass_sems.at[zh])
            share(relp, zh, qs)

    for zh in (1, 0):
        drain(recv_g.at[0 : 8 - zh], line_sems.at[1 + zh])
        for j in range(4):
            k = (zh * 4 + j + 3) % DEPTH
            same, sister = unfold(recv_g[2 * k].astype(F32)), unfold(recv_g[2 * k + 1].astype(F32))
            block = jnp.concatenate([jnp.where(lower, same, sister), jnp.where(lower, sister, same)], axis=0)
            start = spot(0, zh, 3) + j * ROWS
            tab[start : start + ROWS, :] = block.astype(BF16)
        for d in (2, 1, 3):
            n = zh * 3 + d - 1
            across[zh, d] = send(
                piece(tab, 0, zh, 3), piece(tab, 0, zh, d - 1), around[d], 10, across_sems.at[2 + n]
            )
        first_ring(zh, 3)
    for zh in (1, 0):
        for d in (1, 3, 2):
            across[zh, d].wait_recv()
            first_ring(zh, d - 1)
        pass_on(zh, 3)

    step = 512

    def look(state, which, table, spans):
        def tile(t, carry):
            tok = pl.ds(pl.multiple_of(t * step, step), step)
            picked = [
                jnp.dot(which[tok, a : a + n], table[a : a + n, :], preferred_element_type=F32) for a, n in spans
            ]
            state[tok, :] = (state[tok, :].astype(F32) - sum(picked[1:], picked[0])).astype(BF16)
            return carry

        lax.fori_loop(0, tokens // step, tile, 0)

    look(own, hot, tab, [(0, PB)])
    loads[4].wait()
    drain(tab.at[0:PB, :], share_sems.at[0])
    look(oth, hot_sib, tab_sib, [(0, PB)])
    for qs in (0, 2, 1):
        pass_on(1, qs)
    look(own, hot, tab, [(PB + HALF, HALF), (3 * PB + HALF, HALF)])
    for qs in (0, 2, 1):
        pass_on(0, qs)
    look(own, hot, tab, [(PB, HALF), (3 * PB, HALF)])
    last = []

    def hand_over(zh):
        drain(tab.at[0:HALF, :], pass_sems.at[zh])
        start = spot(2, zh, 0)
        last.append(
            send(tab.at[start : start + HALF, :], tab_sib.at[start : start + HALF, :], sibling, 11 + zh, pass_sems.at[2 + zh])
        )

    drain(tab.at[0:PB, :], share_sems.at[1])
    drain(tab.at[0:PB, :], share_sems.at[3])
    hand_over(1)
    look(oth, hot_sib, tab_sib, [(PB, PB), (3 * PB, PB)])
    hand_over(0)
    drain(asg, send_sems.at[0])
    drain(own, send_sems.at[1])
    drain(send_p, send_sems.at[2])
    drain(old_sib, send_sems.at[3])
    drain(send_q.at[:, 0 : 3 * PIECE, :], send_sems.at[4])
    drain(send_z.at[1:], send_sems.at[5])
    drain(send_z.at[1:], send_sems.at[6])
    drain(tab.at[0 : 2 * PB, :], send_sems.at[8])
    drain(tab.at[0 : 6 * PIECE, :], send_sems.at[10])

    def finish(state, which, table, columns):
        def tile(t, carry):
            tok = pl.ds(pl.multiple_of(t * step, step), step)
            picked = jnp.dot(which[tok, 2 * PB : 3 * PB], table[2 * PB : 3 * PB, :], preferred_element_type=F32)
            out[tok, columns] = (state[tok, :].astype(F32) - picked).astype(BF16)
            return carry

        lax.fori_loop(0, tokens // step, tile, 0)

    finish(own, hot, tab, mine)
    for copy in last:
        copy.wait_recv()
    finish(oth, hot_sib, tab_sib, theirs)

    away = lax.rem(core + r, 2) * 2
    base = HALF + (HOME - 4) * ROWS
    a = base + swap * (3 - away) * PIECE + core * (away * PB + 3 * PIECE)
    b = base + core * (3 - away) * PIECE + swap * (away * PB + 3 * PIECE)
    new_out[:, mine] = tab[pl.ds(pl.multiple_of(a, ROWS), ROWS), :]
    new_out[:, theirs] = tab_sib[pl.ds(pl.multiple_of(b, ROWS), ROWS), :]
    drain(tab.at[0 : 3 * PB, :], send_sems.at[7])
    drain(tab.at[0:PB, :], send_sems.at[9])
    for copy in last:
        copy.wait_send()


def body(embeddings, assignments, old_centroids, old_counts):
    tokens, width = embeddings.shape
    half, table = width // 2, RING * PB
    vmem, dma = pltpu.VMEM, pltpu.SemaphoreType.DMA
    operands = (embeddings, assignments.reshape(1, tokens), old_centroids, old_counts.reshape(1, ROWS))
    hbm = pl.BlockSpec(memory_space=pltpu.HBM)
    return pl.pallas_call(
        kernel,
        out_shape=(vmem((tokens, width), BF16), vmem((ROWS, width), BF16)),
        in_specs=[hbm] * 4,
        out_specs=(pl.BlockSpec(memory_space=vmem), pl.BlockSpec(memory_space=vmem)),
        scratch_shapes=[
            vmem((tokens, half), BF16),
            vmem((tokens, half), BF16),
            vmem((tokens, half), BF16),
            vmem((1, tokens), I32),
            vmem((1, tokens), I32),
            vmem((ROWS, width), BF16),
            vmem((1, ROWS), I32),
            vmem((ROWS, width), F32),
            vmem((TOP, width), F32),
            vmem((PB, 128), I16),
            vmem((HALF, 2 * tokens), BF16),
            vmem((6, HALF, half), BF16),
            vmem((6, HALF, half), BF16),
            vmem((4, HALF, half), F32),
            vmem((2, HALF, half), BF16),
            vmem((2, HALF, half), BF16),
            vmem((2 * DEPTH, ROWS, half // 2), BF16),
            vmem((2 * DEPTH, ROWS, half // 2), BF16),
            vmem((2, ROWS, half // 2), BF16),
            vmem((2 * DEPTH, ROWS, half // 2), BF16),
            vmem((table, half), BF16),
            vmem((table, half), BF16),
            vmem((tokens, 128), I16),
            vmem((tokens, table), BF16),
            vmem((tokens, table), BF16),
            dma((5,)),
            dma((13,)),
            dma((4,)),
            dma((8,)),
            dma((2,)),
            dma((8,)),
            dma((8,)),
            dma((3,)),
            dma((16,)),
            dma((4,)),
            dma((4,)),
        ],
        compiler_params=pltpu.CompilerParams(
            collective_id=0, has_side_effects=True, vmem_limit_bytes=58 * 1024 * 1024
        ),
        cost_estimate=pl.CostEstimate(flops=8 * 2**30, bytes_accessed=4 * 2**20, transcendentals=0),
    )(*[pltpu.with_memory_space_constraint(operand, pltpu.HBM) for operand in operands])


def solution(mesh):
    placed = (P(("corpus", "rep"), None), P(("corpus", "rep")), P("corpus", None), P("corpus"))
    return jax.shard_map(
        body,
        mesh=mesh,
        in_specs=placed,
        out_specs=(P(("corpus", "rep"), None), P("corpus", None)),
        check_vma=False,
    )
```
